256 devices in a mesh: dp: 32 (over x, y, core), proto: 8 (over z).
Axes of the slice: x: 4, y: 4, z: 8, core: 2. Of those that a mesh axis runs over, the one named last changes fastest.
Arguments:
- teacher_features: bfloat16 [8192, 256], P('dp')
- teacher_protos: bfloat16 [256, 65536], P(None, 'proto')
- student_features: bfloat16 [8192, 256], P('dp')
- student_protos: bfloat16 [256, 65536], P(None, 'proto')
- student_source: int32 [8192], P('dp'), may hold values from 0 to 8191, as said below
Outputs:
- loss: float32 [], replicated
- grad_features: float32 [8192, 256], P('dp')
- grad_protos: float32 [256, 65536], P('dp', 'proto')
The draws below stay inside these ranges and needn't reach their ends.
Inputs may be any that keep to these rules, and one draw needn't show every extreme that they name: `student_source`: A permutation of the teacher rows; the student rows of each index of dp take exactly 8 crops from the teacher rows of every index of dp.
All inputs are finite; a program needn't handle non-finite values.
Results may differ from the reference program's by a relative error of at most 0.00095.
The reference program's roundings to bfloat16 on the way count: a program that leaves them out, or rounds other values in their place, can miss the bound.
Values may be sent and summed in bfloat16 or wider, within the bound.
No kernel may reach another device: no remote copies, remote signals or barrier semaphores. Data moves between devices by JAX's collectives and lax.ppermute only.
A program may use at most 128 MiB of HBM per device.

```python
import math
import jax
import jax.numpy as jnp
from jax import lax

BOTTLENECK = 256
PROTOS = 65536
CROPS_DEV = 256
ITERS = 3
CROPS = 8192


def dim_scale(key):
    return jnp.exp(jax.random.uniform(jax.random.fold_in(key, 101), (BOTTLENECK,), jnp.float32) * math.log(1000.0))


def draw_teacher_features(key, part):
    scales = dim_scale(key)
    key = jax.random.fold_in(key, 1)
    noise = jax.random.normal(key, (CROPS, BOTTLENECK), jnp.float32)
    return (noise * scales[None, :] / 4000.0).astype(jnp.bfloat16)


def draw_student_features(key, part):
    scales = dim_scale(key)
    key = jax.random.fold_in(key, 2)
    noise = jax.random.normal(key, (CROPS, BOTTLENECK), jnp.float32)
    return (noise * scales[None, :] / 4000.0).astype(jnp.bfloat16)


def draw_teacher_protos(key, part):
    scales = dim_scale(key)
    key = jax.random.fold_in(key, 3)
    noise = jax.random.normal(key, (BOTTLENECK, PROTOS), jnp.float32)
    return (noise * scales[:, None] / 1000.0).astype(jnp.bfloat16)


def draw_student_protos(key, part):
    scales = dim_scale(key)
    key = jax.random.fold_in(key, 4)
    noise = jax.random.normal(key, (BOTTLENECK, PROTOS), jnp.float32)
    return (noise * scales[:, None] / 1000.0).astype(jnp.bfloat16)


def draw_student_source(key, part):
    key = jax.random.fold_in(key, 5)
    row_count = CROPS_DEV
    part_count = CROPS // CROPS_DEV
    slot_rows = row_count // part_count
    teacher_key, student_key = jax.random.split(key)
    teacher_order = jax.vmap(lambda sub: jax.random.permutation(sub, row_count))(jax.random.split(teacher_key, part_count))
    crop_index = teacher_order + (jnp.arange(part_count, dtype=jnp.int32) * row_count)[:, None]
    grouped = crop_index.reshape(part_count, part_count, slot_rows).transpose(1, 0, 2).reshape(part_count, row_count)
    student_order = jax.vmap(lambda sub: jax.random.permutation(sub, row_count))(jax.random.split(student_key, part_count))
    placed = jnp.take_along_axis(grouped, student_order, axis=1)
    return placed.reshape(-1).astype(jnp.int32)


def setup_inputs(seed: int = 0) -> dict:
    splits = jax.random.split(jax.random.key(seed), 6)
    teacher_features = draw_teacher_features(jax.random.fold_in(splits[5], 71), 0)
    teacher_protos = draw_teacher_protos(jax.random.fold_in(splits[5], 71), 0)
    student_features = draw_student_features(jax.random.fold_in(splits[5], 71), 0)
    student_protos = draw_student_protos(jax.random.fold_in(splits[5], 71), 0)
    student_source = draw_student_source(jax.random.fold_in(splits[5], 71), 0)
    return dict(teacher_features=teacher_features, teacher_protos=teacher_protos, student_features=student_features, student_protos=student_protos, student_source=student_source)


TEACHER_TEMP = 0.04
STUDENT_TEMP = 0.1
NORM_EPSILON = 1e-06

def unit_rows(values):
    floats = values.astype(jnp.float32)
    norms = jnp.sqrt(lax.optimization_barrier(jnp.sum(floats * floats, axis=1, keepdims=True)) + NORM_EPSILON)
    return (floats / norms, norms)

def unit_columns(values):
    floats = values.astype(jnp.float32)
    norms = jnp.sqrt(lax.optimization_barrier(jnp.sum(floats * floats, axis=0, keepdims=True)) + NORM_EPSILON)
    return (floats / norms, norms)

def reference(teacher_features, teacher_protos, student_features, student_protos, student_source):
    teacher_unit, _ = unit_rows(teacher_features)
    teacher_hat = teacher_unit.astype(jnp.bfloat16)
    teacher_dirs, _ = unit_columns(teacher_protos)
    teacher_dirs = teacher_dirs.astype(jnp.bfloat16)
    student_unit, student_norm = unit_rows(student_features)
    student_hat = student_unit.astype(jnp.bfloat16)
    student_dirs, dir_norm = unit_columns(student_protos)
    dirs_hat = student_dirs.astype(jnp.bfloat16)
    block_width = min(PROTOS, 4096)
    block_count = PROTOS // block_width

    def split_blocks(matrix):
        return matrix.reshape(matrix.shape[0], block_count, block_width).transpose(1, 0, 2)
    teacher_blocks = split_blocks(teacher_dirs)
    student_blocks = split_blocks(dirs_hat)
    unit_blocks = split_blocks(student_dirs)
    norm_blocks = split_blocks(dir_norm)

    def teacher_exp(block):
        return jnp.exp(jnp.dot(teacher_hat, block, preferred_element_type=jnp.float32) / TEACHER_TEMP)
    row_scale = jnp.ones((CROPS,), jnp.float32)
    col_scale = jnp.ones((block_count, block_width), jnp.float32)
    for sweep in range(ITERS):

        def column_mass(block, scale_rows=row_scale):
            return lax.optimization_barrier(jnp.sum(teacher_exp(block) * scale_rows[:, None], axis=0))
        col_scale = 1.0 / (PROTOS * lax.map(column_mass, teacher_blocks))

        def add_rows(running, packed):
            block, scale_cols = packed
            return (running + lax.optimization_barrier(jnp.sum(teacher_exp(block) * scale_cols[None, :], axis=1)), None)
        row_mass, _ = lax.scan(add_rows, jnp.zeros((CROPS,), jnp.float32), (teacher_blocks, col_scale))
        row_scale = 1.0 / (CROPS * row_mass)

    def targets_of(block, scale_cols):
        mass = teacher_exp(block) * row_scale[:, None] * scale_cols[None, :]
        return (mass * CROPS).astype(jnp.bfloat16)[student_source].astype(jnp.float32)

    def first_pass(running, packed):
        block, scale_cols, student_block = packed
        target_values = targets_of(block, scale_cols)
        scores = jnp.dot(student_hat, student_block, preferred_element_type=jnp.float32) / STUDENT_TEMP
        return ((running[0] + lax.optimization_barrier(jnp.sum(jnp.exp(scores), axis=1)), running[1] + lax.optimization_barrier(jnp.sum(target_values, axis=1)), running[2] + lax.optimization_barrier(jnp.sum(target_values * scores, axis=1))), None)
    zero_rows = jnp.zeros((CROPS,), jnp.float32)
    (exp_total, target_total, cross), _ = lax.scan(first_pass, (zero_rows, zero_rows, zero_rows), (teacher_blocks, col_scale, student_blocks))
    log_total = jnp.log(exp_total)
    loss = jnp.sum(target_total * log_total - cross) / CROPS

    def second_pass(feature_grad, packed):
        block, scale_cols, student_block, unit_block, norm_block = packed
        target_values = targets_of(block, scale_cols)
        cosine = jnp.dot(student_hat, student_block, preferred_element_type=jnp.float32)
        scores = cosine / STUDENT_TEMP
        probs = jnp.exp(scores - log_total[:, None])
        score_grad = ((probs * target_total[:, None] - target_values) / STUDENT_TEMP).astype(jnp.bfloat16)
        feature_grad = feature_grad + lax.dot_general(score_grad, student_block, (((1,), (1,)), ((), ())), preferred_element_type=jnp.float32)
        weight_grad = lax.dot_general(student_hat, score_grad, (((0,), (0,)), ((), ())), preferred_element_type=jnp.float32)
        column_stat = lax.optimization_barrier(jnp.sum(score_grad.astype(jnp.float32) * cosine, axis=0))
        return (feature_grad, (weight_grad - unit_block * column_stat[None, :]) / norm_block)
    feature_grad, grad_blocks = lax.scan(second_pass, jnp.zeros((CROPS, BOTTLENECK), jnp.float32), (teacher_blocks, col_scale, student_blocks, unit_blocks, norm_blocks))
    grad_protos = grad_blocks.transpose(1, 0, 2).reshape(BOTTLENECK, PROTOS)
    along = lax.optimization_barrier(jnp.sum(student_unit * feature_grad, axis=1, keepdims=True))
    grad_features = (feature_grad - student_unit * along) / student_norm
    return (loss, grad_features, grad_protos)
```

```python
import jax
import jax.numpy as jnp
from jax import lax
from jax.sharding import Mesh, PartitionSpec as P

PROTOS = 65536
CROPS = 8192
ITERS = 3
NX, NY, NC, NZ = 4, 4, 2, 8
DP = ("x", "y", "c")

TEACHER_TEMP = 0.04
STUDENT_TEMP = 0.1
NORM_EPSILON = 1e-06


def unit_rows(values):
    floats = values.astype(jnp.float32)
    norms = jnp.sqrt(jnp.sum(floats * floats, axis=1, keepdims=True) + NORM_EPSILON)
    return (floats / norms, norms)


def unit_columns(values):
    floats = values.astype(jnp.float32)
    norms = jnp.sqrt(jnp.sum(floats * floats, axis=0, keepdims=True) + NORM_EPSILON)
    return (floats / norms, norms)


def shift(v, axis, size, step):
    return lax.ppermute(v, axis, [(i, (i + step) % size) for i in range(size)])


def gather_y(v):
    return jnp.concatenate([v] + [shift(v, "y", NY, s) for s in range(1, NY)], axis=0)


def flip_blocks(v, y):
    blocks = v.reshape((NY, -1) + v.shape[1:])
    return blocks[(y - jnp.arange(NY)) % NY].reshape(v.shape)


def sum_rows(v):
    n = NY * NZ
    got = lax.all_to_all(jnp.broadcast_to(v[None], (n,) + v.shape), ("y", "z"), 0, 0, tiled=True)
    return jnp.sum(got, axis=0)


def sum_columns(v):
    v = v + shift(v, "c", NC, 1)
    return v + (shift(v, "x", NX, 1) + shift(v, "x", NX, 2) + shift(v, "x", NX, 3))


def body(teacher_features, teacher_protos, student_features, student_protos, student_source):
    rows = student_source.shape[0]
    parts = NX * NY * NC
    width = teacher_protos.shape[1] // NY
    y = lax.axis_index("y")
    c = lax.axis_index("c")

    owner = student_source // rows
    local = student_source % rows
    order = jnp.arange(rows)
    rank = jnp.sum((owner[:, None] == owner[None, :]) & (order[None, :] < order[:, None]), axis=1)
    slot = owner * (rows // parts) + rank
    place = slot[:, None] == order[None, :]
    request = jnp.sum(jnp.where(place, local[:, None], 0), axis=0).astype(jnp.int32)
    asked = lax.all_to_all(request.reshape(parts, rows // parts), DP, 0, 0, tiled=True).reshape(-1)
    pick = (asked[:, None] == order[None, :]).astype(jnp.bfloat16)
    parcel = jnp.dot(pick, teacher_features, preferred_element_type=jnp.float32).astype(jnp.bfloat16)
    arrived = lax.all_to_all(parcel.reshape(parts, rows // parts, -1), DP, 0, 0, tiled=True)
    matched = jnp.dot(
        place.astype(jnp.bfloat16), arrived.reshape(rows, -1), preferred_element_type=jnp.float32
    ).astype(jnp.bfloat16)

    teacher_rows = gather_y(teacher_features)
    student_rows = gather_y(student_features)
    matched_rows = gather_y(matched)

    protos_t = lax.dynamic_slice_in_dim(teacher_protos, y * width, width, 1)
    protos_s = lax.dynamic_slice_in_dim(student_protos, y * width, width, 1)
    teacher_dirs = unit_columns(protos_t)[0].astype(jnp.bfloat16)
    student_dirs, dir_norm = unit_columns(protos_s)
    dirs_hat = student_dirs.astype(jnp.bfloat16)
    student_unit, student_norm = unit_rows(student_rows)
    student_hat = student_unit.astype(jnp.bfloat16)

    def teacher_mass(features):
        unit = unit_rows(features)[0].astype(jnp.bfloat16)
        return jnp.exp(jnp.dot(unit, teacher_dirs, preferred_element_type=jnp.float32) / TEACHER_TEMP)

    mass = teacher_mass(teacher_rows)
    mass_s = teacher_mass(matched_rows)
    cosine = jnp.dot(student_hat, dirs_hat, preferred_element_type=jnp.float32)
    scores = cosine / STUDENT_TEMP
    exp_part = jnp.sum(jnp.exp(scores), axis=1)

    column = sum_columns(jnp.sum(mass, axis=0))
    for sweep in range(ITERS - 1):
        col_scale = 1.0 / (PROTOS * column)
        row = flip_blocks(sum_rows(flip_blocks(jnp.sum(mass * col_scale[None, :], axis=1), y)), y)
        row_scale = 1.0 / (CROPS * row)
        column = sum_columns(jnp.sum(mass * row_scale[:, None], axis=0))
    col_scale = 1.0 / (PROTOS * column)
    part = flip_blocks(jnp.sum(mass_s * col_scale[None, :], axis=1), y)
    part = sum_rows(jnp.concatenate([part, flip_blocks(exp_part, y)]))
    row_scale = 1.0 / (CROPS * flip_blocks(part[: NY * rows], y))
    log_total = jnp.log(flip_blocks(part[NY * rows :], y))
    targets = (mass_s * row_scale[:, None] * col_scale[None, :] * CROPS).astype(jnp.bfloat16)
    target_values = targets.astype(jnp.float32)
    cross = jnp.sum(target_values * scores)
    part = flip_blocks(jnp.sum(target_values, axis=1), y)
    part = sum_rows(jnp.concatenate([part, jnp.full((128,), cross)]))
    target_total = flip_blocks(part[: NY * rows], y)
    loss = jnp.sum(target_total * log_total) - part[NY * rows]
    loss = sum_columns(jnp.full((128,), loss))[0] / CROPS

    probs = jnp.exp(scores - log_total[:, None])
    score_grad = ((probs * target_total[:, None] - target_values) / STUDENT_TEMP).astype(jnp.bfloat16)
    feature = lax.dot_general(
        score_grad, dirs_hat, (((1,), (1,)), ((), ())), preferred_element_type=jnp.float32
    )
    along = jnp.sum(student_unit * feature, axis=1, keepdims=True)
    feature = (feature - student_unit * along) / student_norm
    feature = flip_blocks(feature, y).reshape(NY * NZ, rows // NZ, -1)
    feature = jnp.sum(lax.all_to_all(feature, ("y", "z"), 0, 0, tiled=True), axis=0)
    feature = jnp.broadcast_to(feature[None], (NZ,) + feature.shape)
    grad_features = lax.all_to_all(feature, "z", 0, 0, tiled=True).reshape(rows, -1)

    weight = lax.dot_general(
        student_hat, score_grad, (((0,), (0,)), ((), ())), preferred_element_type=jnp.float32
    )
    stat = jnp.sum(score_grad.astype(jnp.float32) * cosine, axis=0)
    weight = (weight - student_dirs * stat[None, :]) / dir_norm
    share = weight.shape[0] // parts
    weight = weight.reshape(NX * NY, NC, share, width)
    keep = lax.dynamic_index_in_dim(weight, c, 1, keepdims=False)
    give = lax.dynamic_index_in_dim(weight, 1 - c, 1, keepdims=False)
    weight = keep + shift(give, "c", NC, 1)
    weight = lax.all_to_all(weight, ("x", "y"), 0, 0, tiled=True)
    weight = jnp.sum(weight.reshape(NX, NY, share, width), axis=0)
    grad_protos = weight.transpose(1, 0, 2).reshape(share, NY * width)
    return (loss, grad_features, grad_protos)


def solution(mesh):
    return jax.shard_map(
        body,
        mesh=Mesh(mesh.devices.reshape(NX, NY, NC, NZ), ("x", "y", "c", "z")),
        in_specs=(P(DP, None), P(None, "z"), P(DP, None), P(None, "z"), P(DP)),
        out_specs=(P(), P(DP, None), P(DP, "z")),
        check_vma=False,
    )
```

```python
import functools

import jax
import jax.numpy as jnp
from jax import lax
from jax.experimental import pallas as pl
from jax.experimental.pallas import tpu as pltpu
from jax.sharding import Mesh, PartitionSpec as P

PROTOS = 65536
CROPS = 8192
ITERS = 3
NX, NY, NC, NZ = 4, 4, 2, 8
DP = ("x", "y", "c")
PARTS = NX * NY * NC
ROWS = CROPS // PARTS
SLOT = ROWS // PARTS
DEPTH = 256
GROUP = NY * ROWS
WIDTH = PROTOS // (NY * NZ)
CHUNK = 1024
LANES = 128
RB = GROUP // LANES
KB = WIDTH // LANES
PEERS = NY * NZ

TEACHER_TEMP = 0.04
STUDENT_TEMP = 0.1
NORM_EPSILON = 1e-06
F32 = jnp.float32
BF16 = jnp.bfloat16

WHOLE = pl.BlockSpec(memory_space=pltpu.VMEM)
PARAMS = pltpu.CompilerParams(vmem_limit_bytes=24 << 20)
ROW_BLOCK = pl.BlockSpec((ROWS, DEPTH), lambda j, s: (0, 0))


def proto_block(chunk):
    return pl.BlockSpec((DEPTH, chunk), lambda j, s: (0, s[1] * (WIDTH // chunk) + j))


def call(kernel, out_shape, *args):
    return pl.pallas_call(
        kernel,
        in_specs=[WHOLE] * len(args),
        out_specs=jax.tree.map(lambda _: WHOLE, out_shape),
        out_shape=out_shape,
        compiler_params=PARAMS,
    )(*args)


def shape(dims, dtype=F32):
    return jax.ShapeDtypeStruct(dims, dtype)


def unit(values, axis):
    floats = values.astype(F32)
    norms = jnp.sqrt(jnp.sum(floats * floats, axis=axis, keepdims=True) + NORM_EPSILON)
    return floats / norms, norms


def own_rows(s, b):
    return pl.ds(pl.multiple_of(lax.rem(s[1] - b + NY, NY) * ROWS, ROWS), ROWS)


def block(rb):
    return slice(rb * LANES, (rb + 1) * LANES)


def lanes_to_rows(row):
    return jnp.broadcast_to(row, (LANES, LANES)).T


def fold_lanes(values):
    return functools.reduce(jnp.add, [values[:, block(k)] for k in range(values.shape[1] // LANES)])


def rows_to_lanes(values):
    return jnp.sum(values.T, axis=0, keepdims=True)


def dot(a, b):
    return jnp.dot(a, b, preferred_element_type=F32)


def exclusive_counts(marks):
    n = marks.shape[1]
    before = lax.broadcasted_iota(jnp.int32, (n, n), 0) < lax.broadcasted_iota(jnp.int32, (n, n), 1)
    return dot(marks.astype(BF16), before.astype(BF16))


def mass_kernel(s, r0, r1, r2, r3, protos, mass, column, units):
    j = pl.program_id(0)

    @pl.when(j == 0)
    def _():
        for b, rows in enumerate((r0, r1, r2, r3)):
            units[own_rows(s, b), :] = unit(rows[...], 1)[0].astype(BF16)

    dirs = unit(protos[...], 0)[0].astype(BF16)
    cols = pl.ds(pl.multiple_of(j * CHUNK, CHUNK), CHUNK)
    total = jnp.zeros((8, CHUNK), F32)
    for rb in range(RB):
        part = jnp.exp(dot(units[block(rb), :], dirs) * (1.0 / TEACHER_TEMP))
        mass[block(rb), cols] = part
        total = total + jnp.sum(part.reshape(LANES // 8, 8, CHUNK), axis=0)
    total = jnp.sum(total, axis=0, keepdims=True)
    for k in range(CHUNK // LANES):
        column[k : k + 1, :] = total[:, block(k)]


def teacher_mass(s, rows, protos):
    return pl.pallas_call(
        mass_kernel,
        grid_spec=pltpu.PrefetchScalarGridSpec(
            num_scalar_prefetch=1,
            grid=(WIDTH // CHUNK,),
            in_specs=[ROW_BLOCK] * NY + [proto_block(CHUNK)],
            out_specs=[WHOLE, pl.BlockSpec((CHUNK // LANES, LANES), lambda j, s: (j, 0))],
            scratch_shapes=[pltpu.VMEM((GROUP, DEPTH), BF16)],
        ),
        out_shape=[shape((GROUP, WIDTH)), shape((KB, LANES))],
        compiler_params=PARAMS,
    )(s, *rows, protos)


def col_scale(pieces):
    return 1.0 / (PROTOS * (pieces[0][...] + pieces[1][...] + pieces[2][...] + pieces[3][...]))


def row_part(mass, scale, rb):
    total = jnp.zeros((LANES, LANES), F32)
    for k in range(KB):
        total = total + mass[block(rb), block(k)] * scale[k : k + 1, :]
    return rows_to_lanes(total)


def copies(out):
    value = out[0]
    for i in range(1, PEERS):
        out[i] = value


def row_kernel(mass, a0, a1, a2, a3, out):
    scale = col_scale((a0, a1, a2, a3))
    for rb in range(RB):
        out[0, rb : rb + 1, :] = row_part(mass, scale, rb)
    copies(out)


def last_row_kernel(mass, a0, a1, a2, a3, exps, out):
    scale = col_scale((a0, a1, a2, a3))
    for rb in range(RB):
        out[0, rb : rb + 1, :] = row_part(mass, scale, rb)
    out[0, RB : 2 * RB, :] = exps[...]
    copies(out)


def column_kernel(mass, got, out):
    scale = 1.0 / (CROPS * jnp.sum(got[...], axis=0))
    totals = [jnp.zeros((8, LANES), F32) for _ in range(KB)]
    for rb in range(RB):
        factor = lanes_to_rows(scale[rb : rb + 1, :])
        for k in range(KB):
            part = mass[block(rb), block(k)] * factor
            totals[k] = totals[k] + jnp.sum(part.reshape(LANES // 8, 8, LANES), axis=0)
    for k in range(KB):
        out[k : k + 1, :] = jnp.sum(totals[k], axis=0, keepdims=True)


def student_kernel(s, r0, r1, r2, r3, protos, exps, hat, sums):
    j = pl.program_id(0)

    @pl.when(j == 0)
    def _():
        sums[...] = jnp.zeros_like(sums)
        for b, rows in enumerate((r0, r1, r2, r3)):
            hat[own_rows(s, b), :] = unit(rows[...], 1)[0].astype(BF16)

    dirs = unit(protos[...], 0)[0].astype(BF16)
    for rb in range(RB):
        part = jnp.exp(dot(hat[block(rb), :], dirs) * (1.0 / STUDENT_TEMP))
        sums[block(rb), :] = sums[block(rb), :] + fold_lanes(part)

    @pl.when(j == pl.num_programs(0) - 1)
    def _():
        for rb in range(RB):
            exps[rb : rb + 1, :] = rows_to_lanes(sums[block(rb), :])


def student_exps(s, rows, protos):
    return pl.pallas_call(
        student_kernel,
        grid_spec=pltpu.PrefetchScalarGridSpec(
            num_scalar_prefetch=1,
            grid=(WIDTH // CHUNK,),
            in_specs=[ROW_BLOCK] * NY + [proto_block(CHUNK)],
            out_specs=[WHOLE, WHOLE],
            scratch_shapes=[pltpu.VMEM((GROUP, LANES), F32)],
        ),
        out_shape=[shape((RB, LANES)), shape((GROUP, DEPTH), BF16)],
        compiler_params=PARAMS,
    )(s, *rows, protos)


def pick_kernel(s, source, features, out):
    me = (s[0] * NY + s[1]) * NC + s[2]
    marks = lax.shift_right_logical(source[...], 8) == me
    local = jnp.bitwise_and(source[...], ROWS - 1).astype(F32)
    counts = exclusive_counts(jnp.where(marks, 1.0, 0.0))
    counts = jnp.where(marks, counts, -1.0)
    rank = lax.broadcasted_iota(jnp.int32, (PARTS, SLOT, ROWS), 1).astype(F32)
    shown = jnp.where(counts[:, None, :] == rank, local[:, None, :], 0.0)
    asked = jnp.sum(shown, axis=2, keepdims=True)
    lane = lax.broadcasted_iota(jnp.int32, (PARTS, SLOT, ROWS), 2).astype(F32)
    pick = jnp.where(asked == lane, 1.0, 0.0).reshape(ROWS, ROWS).astype(BF16)
    rows = dot(pick, features[...])
    for x in range(NX):
        for c in range(NC):
            parts = []
            for y in range(NY):
                e = ((x * NY + y) * NC + c) * SLOT
                parts.append(rows[e : e + SLOT, :])
            parcel = jnp.concatenate(parts, axis=0).astype(BF16)
            for y in range(NY):
                out[(x * NY + y) * NC + c] = parcel


def pick_rows(s, source, features):
    return pl.pallas_call(
        pick_kernel,
        in_specs=[pl.BlockSpec(memory_space=pltpu.SMEM), WHOLE, WHOLE],
        out_specs=WHOLE,
        out_shape=shape((PARTS, NY * SLOT, DEPTH), BF16),
        compiler_params=PARAMS,
    )(s, source, features)


def matched_kernel(s, source, arrived, protos, mass, units):
    j = pl.program_id(0)

    @pl.when(j == 0)
    def _():
        index = lax.broadcasted_iota(jnp.int32, (PARTS, ROWS), 0)
        part = lax.broadcasted_iota(jnp.int32, (PARTS, ROWS), 0)
        slot = lax.broadcasted_iota(jnp.int32, (ROWS, ROWS), 0).astype(F32)
        rows = arrived[...].astype(F32)
        for y in range(NY):
            e = (s[0] * NY + y) * NC + s[2]
            mine = jnp.sum(jnp.where(index == e, source[...], 0), axis=0, keepdims=True)
            owner = lax.shift_right_logical(mine, 8)
            marks = jnp.where(part == owner, 1.0, 0.0)
            rank = jnp.sum(marks * exclusive_counts(marks), axis=0, keepdims=True)
            place = jnp.where(slot == owner.astype(F32) * SLOT + rank, 1.0, 0.0).astype(BF16)
            came = rows[:, y * SLOT : (y + 1) * SLOT, :].reshape(ROWS, DEPTH).astype(BF16)
            matched = lax.dot_general(place, came, (((0,), (0,)), ((), ())), preferred_element_type=F32)
            units[y * ROWS : (y + 1) * ROWS, :] = unit(matched, 1)[0].astype(BF16)

    dirs = unit(protos[...], 0)[0].astype(BF16)
    cols = pl.ds(pl.multiple_of(j * CHUNK, CHUNK), CHUNK)
    for rb in range(RB):
        mass[block(rb), cols] = jnp.exp(dot(units[block(rb), :], dirs) * (1.0 / TEACHER_TEMP))


def matched_mass(s, source, arrived, protos):
    return pl.pallas_call(
        matched_kernel,
        grid_spec=pltpu.PrefetchScalarGridSpec(
            num_scalar_prefetch=1,
            grid=(WIDTH // CHUNK,),
            in_specs=[WHOLE, WHOLE, proto_block(CHUNK)],
            out_specs=WHOLE,
            scratch_shapes=[pltpu.VMEM((GROUP, DEPTH), BF16)],
        ),
        out_shape=shape((GROUP, WIDTH)),
        compiler_params=PARAMS,
    )(s, source, arrived, protos)


def target_kernel(s, mass, a0, a1, a2, a3, got, hat, protos, targets, exps, out, sums, cross):
    j = pl.program_id(0)
    n = CHUNK // LANES

    @pl.when(j == 0)
    def _():
        sums[...] = jnp.zeros_like(sums)
        cross[...] = jnp.zeros_like(cross)
        exps[...] = jnp.sum(got[...], axis=0)

    dirs = unit(protos[...], 0)[0].astype(BF16)
    rows = pl.ds(pl.multiple_of(j * n, n), n)
    scale = 1.0 / (PROTOS * (a0[rows, :] + a1[rows, :] + a2[rows, :] + a3[rows, :]))
    row_scale = 1.0 / (CROPS * exps[:RB, :])
    for rb in range(RB):
        factor = lanes_to_rows(row_scale[rb : rb + 1, :])
        scores = dot(hat[block(rb), :], dirs) * (1.0 / STUDENT_TEMP)
        total = jnp.zeros((LANES, LANES), F32)
        crossed = jnp.zeros((LANES, LANES), F32)
        for k in range(n):
            cols = pl.ds(pl.multiple_of(j * CHUNK + k * LANES, LANES), LANES)
            value = (mass[block(rb), cols] * factor * scale[k : k + 1, :] * CROPS).astype(BF16)
            targets[block(rb), cols] = value
            value = value.astype(F32)
            total = total + value
            crossed = crossed + value * scores[:, block(k)]
        sums[block(rb), :] = sums[block(rb), :] + total
        cross[...] = cross[...] + crossed

    @pl.when(j == pl.num_programs(0) - 1)
    def _():
        loss = jnp.zeros((1, LANES), F32)
        for rb in range(RB):
            total = rows_to_lanes(sums[block(rb), :])
            out[0, rb : rb + 1, :] = total
            loss = loss + total * jnp.log(exps[RB + rb : RB + rb + 1, :])
        loss = loss - jnp.sum(cross[...], axis=0, keepdims=True)
        out[0, RB : 2 * RB, :] = jnp.broadcast_to(loss, (RB, LANES))
        copies(out)


def make_targets(s, mass, pieces, got, hat, protos):
    return pl.pallas_call(
        target_kernel,
        grid_spec=pltpu.PrefetchScalarGridSpec(
            num_scalar_prefetch=1,
            grid=(WIDTH // CHUNK,),
            in_specs=[WHOLE] * 7 + [proto_block(CHUNK)],
            out_specs=[WHOLE] * 3,
            scratch_shapes=[pltpu.VMEM((GROUP, LANES), F32), pltpu.VMEM((LANES, LANES), F32)],
        ),
        out_shape=[
            shape((GROUP, WIDTH), BF16),
            shape((2 * RB, LANES)),
            shape((PEERS, 2 * RB, LANES)),
        ],
        compiler_params=PARAMS,
    )(s, mass, *pieces, got, hat, protos)


def grad_kernel(s, targets, exps, got, hat, protos, r0, r1, r2, r3, feature, keep, give, loss, factor, grads, turned):
    j = pl.program_id(0)

    @pl.when(j == 0)
    def _():
        totals = jnp.sum(got[...], axis=0)
        loss[...] = totals[RB:, :]
        scale = totals[:RB, :] / exps[RB:, :]
        for rb in range(RB):
            factor[block(rb), :] = lanes_to_rows(scale[rb : rb + 1, :])
        turned[...] = hat[...].astype(F32).T.astype(BF16)
        feature[...] = jnp.zeros_like(feature)

    dirs, norms = unit(protos[...], 0)
    dirs_hat = dirs.astype(BF16)
    for rb in range(RB):
        probs = jnp.exp(dot(hat[block(rb), :], dirs_hat) * (1.0 / STUDENT_TEMP))
        for k in range(GRAD_CHUNK // LANES):
            cols = pl.ds(pl.multiple_of(j * GRAD_CHUNK + k * LANES, LANES), LANES)
            value = probs[:, block(k)] * factor[block(rb), :] - targets[block(rb), cols].astype(F32)
            grads[block(rb), block(k)] = (value * (1.0 / STUDENT_TEMP)).astype(BF16)
    feature[...] = feature[...] + lax.dot_general(
        grads[...], dirs_hat, (((1,), (1,)), ((), ())), preferred_element_type=F32
    )
    weight = dot(turned[...], grads[...])
    stat = jnp.sum(weight * dirs_hat.astype(F32), axis=0, keepdims=True)
    weight = ((weight - dirs * stat) / norms).reshape(NX * NY, NC, DEPTH // PARTS, GRAD_CHUNK)

    @pl.when(s[2] == 0)
    def _():
        keep[...] = weight[:, 0]
        give[...] = weight[:, 1]

    @pl.when(s[2] == 1)
    def _():
        keep[...] = weight[:, 1]
        give[...] = weight[:, 0]

    @pl.when(j == pl.num_programs(0) - 1)
    def _():
        for b, rows in enumerate((r0, r1, r2, r3)):
            units, lengths = unit(rows[...], 1)
            value = feature[own_rows(s, b), :]
            along = jnp.sum(units * value, axis=1, keepdims=True)
            feature[own_rows(s, b), :] = (value - units * along) / lengths


GRAD_CHUNK = 512


def gradients(s, targets, exps, got, hat, protos, rows):
    share = (NX * NY, DEPTH // PARTS, WIDTH)
    part = pl.BlockSpec((NX * NY, DEPTH // PARTS, GRAD_CHUNK), lambda j, s: (0, 0, j))
    return pl.pallas_call(
        grad_kernel,
        grid_spec=pltpu.PrefetchScalarGridSpec(
            num_scalar_prefetch=1,
            grid=(WIDTH // GRAD_CHUNK,),
            in_specs=[WHOLE] * 4 + [proto_block(GRAD_CHUNK)] + [ROW_BLOCK] * NY,
            out_specs=[WHOLE, part, part, WHOLE],
            scratch_shapes=[
                pltpu.VMEM((GROUP, LANES), F32),
                pltpu.VMEM((GROUP, GRAD_CHUNK), BF16),
                pltpu.VMEM((DEPTH, GROUP), BF16),
            ],
        ),
        out_shape=[shape((GROUP, DEPTH)), shape(share), shape(share), shape((RB, LANES))],
        compiler_params=PARAMS,
    )(s, targets, exps, got, hat, protos, *rows)


def shift(v, axis, size, step):
    return lax.ppermute(v, axis, [(i, (i + step) % size) for i in range(size)])


def gather_y(v):
    return [v] + [shift(v, "y", NY, b) for b in range(1, NY)]


def swap_rows(v):
    return lax.all_to_all(v, ("y", "z"), 0, 0, tiled=True)


def column_pieces(v):
    v = v + shift(v, "c", NC, 1)
    return [v] + [shift(v, "x", NX, b) for b in range(1, NX)]


def body(teacher_features, teacher_protos, student_features, student_protos, student_source):
    s = jnp.stack([lax.axis_index(a) for a in DP]).astype(jnp.int32)

    mass, column = teacher_mass(s, gather_y(teacher_features), teacher_protos)
    pieces = column_pieces(column)
    for sweep in range(ITERS - 1):
        parts = call(row_kernel, shape((PEERS, RB, LANES)), mass, *pieces)
        if sweep == 0:
            parts, student_source, student_features = lax.optimization_barrier(
                (parts, student_source, student_features)
            )
        got = swap_rows(parts)
        column = call(column_kernel, shape((KB, LANES)), mass, got)
        pieces = column_pieces(column)

    source = lax.all_to_all(
        jnp.broadcast_to(student_source[None], (PARTS, ROWS)), DP, 0, 0, tiled=True
    )
    parcel = pick_rows(s, source, teacher_features)
    arrived = lax.all_to_all(parcel, DP, 0, 0, tiled=True)
    mass = matched_mass(s, source, arrived, teacher_protos)
    student_rows = gather_y(student_features)
    exps, hat = student_exps(s, student_rows, student_protos)

    got = swap_rows(call(last_row_kernel, shape((PEERS, 2 * RB, LANES)), mass, *pieces, exps))
    targets, exps, parts = make_targets(s, mass, pieces, got, hat, student_protos)
    got = swap_rows(parts)
    feature, keep, give, loss = gradients(s, targets, exps, got, hat, student_protos, student_rows)

    feature = lax.all_to_all(
        feature.reshape(PEERS, GROUP // PEERS, DEPTH), ("y", "z"), 0, 0, tiled=True
    )
    feature = jnp.sum(feature, axis=0)
    feature = jnp.broadcast_to(feature[None], (NZ,) + feature.shape)
    grad_features = lax.all_to_all(feature, "z", 0, 0, tiled=True).reshape(ROWS, DEPTH)

    weight = keep + shift(give, "c", NC, 1)
    weight = lax.all_to_all(weight, ("x", "y"), 0, 0, tiled=True)
    weight = jnp.sum(weight.reshape(NX, NY, DEPTH // PARTS, WIDTH), axis=0)
    grad_protos = weight.transpose(1, 0, 2).reshape(DEPTH // PARTS, NY * WIDTH)

    loss = functools.reduce(jnp.add, column_pieces(loss))
    loss = jnp.sum(loss[0]) / CROPS
    return (loss, grad_features, grad_protos)


def solution(mesh):
    return jax.shard_map(
        body,
        mesh=Mesh(mesh.devices.reshape(NX, NY, NC, NZ), ("x", "y", "c", "z")),
        in_specs=(P(DP, None), P(None, "z"), P(DP, None), P(None, "z"), P(DP)),
        out_specs=(P(), P(DP, None), P(DP, "z")),
        check_vma=False,
    )
```

```python
import functools

import jax
import jax.numpy as jnp
from jax import lax
from jax.experimental import pallas as pl
from jax.experimental.pallas import tpu as pltpu
from jax.sharding import Mesh, PartitionSpec as P

PROTOS = 65536
CROPS = 8192
ITERS = 3
NX, NY, NC, NZ = 4, 4, 2, 8
DP = ("x", "y", "c")
PARTS = NX * NY * NC
ROWS = CROPS // PARTS
SLOT = ROWS // PARTS
DEPTH = 256
GROUP = NY * ROWS
WIDTH = PROTOS // (NY * NZ)
SPAN = PROTOS // NZ
CHUNK = 1024
GRAD_CHUNK = 512
LANES = 128
TILE = 256
RB = GROUP // LANES
KB = WIDTH // LANES
OWN = ROWS // LANES
PEERS = NY * NZ

TEACHER_TEMP = 0.04
STUDENT_TEMP = 0.1
NORM_EPSILON = 1e-06
F32 = jnp.float32
BF16 = jnp.bfloat16

WHOLE = pl.BlockSpec(memory_space=pltpu.VMEM)
PARAMS = pltpu.CompilerParams(vmem_limit_bytes=30 << 20)
COST = pl.CostEstimate(flops=0, bytes_accessed=36000, transcendentals=0)
ROW_BLOCK = pl.BlockSpec((ROWS, DEPTH), lambda j, s: (0, 0))


def proto_block(chunk):
    return split_rows(DEPTH, chunk, 4, lambda j, s: s[1] * (WIDTH // chunk) + j)


def call(kernel, out_shape, *args):
    return pl.pallas_call(
        kernel,
        in_specs=[WHOLE] * len(args),
        out_specs=jax.tree.map(lambda _: WHOLE, out_shape),
        out_shape=out_shape,
        cost_estimate=COST,
        compiler_params=PARAMS,
    )(*args)


class Joined:
    def __init__(self, refs):
        self.refs = refs

    @property
    def shape(self):
        return (sum(r.shape[0] for r in self.refs), self.refs[0].shape[1])

    def __getitem__(self, at):
        return jnp.concatenate([r[at] for r in self.refs], axis=0)


def split_rows(rows, columns, parts, place):
    def spec(r):
        return pl.BlockSpec((rows // parts, columns), lambda j, s: (r, place(j, s)))

    return [spec(r) for r in range(parts)]


def chunked(kernel, steps, in_specs, out_specs, out_shape, scratch=()):
    groups = [spec if isinstance(spec, list) else [spec] for spec in in_specs]

    def regrouped(s, *refs):
        refs, args = list(refs), []
        for spec, group in zip(in_specs, groups):
            mine, refs = refs[: len(group)], refs[len(group) :]
            args.append(Joined(mine) if isinstance(spec, list) else mine[0])
        return kernel(s, *args, *refs)

    run = pl.pallas_call(
        regrouped,
        grid_spec=pltpu.PrefetchScalarGridSpec(
            num_scalar_prefetch=1,
            grid=(steps,),
            in_specs=[spec for group in groups for spec in group],
            out_specs=out_specs,
            scratch_shapes=scratch,
        ),
        out_shape=out_shape,
        cost_estimate=COST,
        compiler_params=PARAMS,
    )

    def apply(s, *args):
        return run(s, *[a for a, group in zip(args, groups, strict=True) for _ in group])

    return apply


def shape(dims, dtype=F32):
    return jax.ShapeDtypeStruct(dims, dtype)


def far(dims, dtype=F32):
    return pltpu.HBM(dims, dtype)


def hbm(v):
    return pltpu.with_memory_space_constraint(v, pltpu.HBM)


def unit(values, axis):
    floats = values.astype(F32)
    inverse = 1.0 / jnp.sqrt(jnp.sum(floats * floats, axis=axis, keepdims=True) + NORM_EPSILON)
    return floats * inverse, inverse


def own_rows(s, b):
    return pl.ds(pl.multiple_of(lax.rem(s[1] - b + NY, NY) * ROWS, ROWS), ROWS)


def block(rb):
    return slice(rb * LANES, (rb + 1) * LANES)


def tile(q):
    return slice(q * TILE, (q + 1) * TILE)


def tile_at(j, q):
    return pl.ds(pl.multiple_of(j * CHUNK + q * TILE, TILE), TILE)


def put_dirs(protos, dirs):
    width = protos.shape[1]
    sums = []
    for k in range(width // LANES):
        floats = protos[:, block(k)].astype(F32)
        parts = (floats * floats).reshape(4, DEPTH // 32, 8, LANES)
        sums.append(jnp.sum(jnp.sum(parts, axis=1), axis=0))
    total = jnp.sum(jnp.concatenate(sums, axis=1), axis=0, keepdims=True)
    inverse = 1.0 / jnp.sqrt(total + NORM_EPSILON)
    for k in range(width // LANES):
        dirs[:, block(k)] = (protos[:, block(k)].astype(F32) * inverse[:, block(k)]).astype(BF16)


def lanes_to_rows(row):
    return jnp.broadcast_to(row, (LANES, LANES)).T


def fold_lanes(values):
    return functools.reduce(jnp.add, [values[:, block(k)] for k in range(values.shape[1] // LANES)])


def rows_to_lanes(values):
    return jnp.sum(values.T, axis=0, keepdims=True)


def dot(a, b):
    return jnp.dot(a, b, preferred_element_type=F32)


def exclusive_counts(marks):
    n = marks.shape[1]
    before = lax.broadcasted_iota(jnp.int32, (n, n), 0) < lax.broadcasted_iota(jnp.int32, (n, n), 1)
    return dot(marks.astype(BF16), before.astype(BF16))


def mass_block(units, dirs, rb):
    return jnp.exp(dot(units[block(rb), :], dirs) * (1.0 / TEACHER_TEMP))


def put_column(column, q, total):
    total = jnp.sum(total, axis=0, keepdims=True)
    for k in range(TILE // LANES):
        row = q * (TILE // LANES) + k
        column[row : row + 1, :] = total[:, block(k)]


def add_rows(total, part):
    return total + jnp.sum(part.reshape(LANES // 8, 8, TILE), axis=0)


def mass_kernel(s, r0, r1, r2, r3, protos, column, dirs, units):
    j = pl.program_id(0)

    @pl.when(j == 0)
    def _():
        for b, rows in enumerate((r0, r1, r2, r3)):
            units[own_rows(s, b), :] = unit(rows[...], 1)[0].astype(BF16)

    put_dirs(protos, dirs)
    for q in range(CHUNK // TILE):
        total = jnp.zeros((8, TILE), F32)
        for rb in range(RB):
            total = add_rows(total, mass_block(units, dirs[:, tile(q)], rb))
        put_column(column, q, total)


COLUMN = pl.BlockSpec((CHUNK // LANES, LANES), lambda j, s: (j, 0))
DIRS_OUT = pl.BlockSpec((DEPTH, CHUNK), lambda j, s: (0, j))
DIRS = split_rows(DEPTH, CHUNK, 4, lambda j, s: j)
ANY = pl.BlockSpec(memory_space=pl.ANY)
GROUP_ROWS = pl.BlockSpec((GROUP, CHUNK), lambda j, s: (0, j))


def teacher_units(s, rows, protos):
    return chunked(
        mass_kernel,
        WIDTH // CHUNK,
        [ROW_BLOCK] * NY + [proto_block(CHUNK)],
        [COLUMN, DIRS_OUT, WHOLE],
        [
            shape((KB, LANES)),
            shape((DEPTH, WIDTH), BF16),
            shape((GROUP, DEPTH), BF16),
        ],
    )(s, *rows, protos)


def again_kernel(s, units, dirs, got, first, *outs):
    j = pl.program_id(0)
    column, factor = outs[-2:]

    @pl.when(j == 0)
    def _():
        scale = 1.0 / (CROPS * jnp.sum(got[...], axis=0))
        for rb in range(RB):
            factor[block(rb), :] = lanes_to_rows(scale[rb : rb + 1, :])

    for q in range(CHUNK // TILE):
        total = jnp.zeros((8, TILE), F32)
        for rb in range(RB):
            part = mass_block(units, dirs[:, tile(q)], rb)
            if len(outs) == 3:
                outs[0][block(rb), tile_at(j, q)] = part
            scaled = [part[:, block(k)] * factor[block(rb), :] for k in range(TILE // LANES)]
            total = add_rows(total, jnp.concatenate(scaled, axis=1))
        put_column(column, q, total)


def columns_again(s, units, dirs, got, first, keep):
    return chunked(
        again_kernel,
        WIDTH // CHUNK,
        [WHOLE, DIRS, WHOLE, ANY],
        [WHOLE] * keep + [COLUMN],
        [shape((GROUP, WIDTH))] * keep + [shape((KB, LANES))],
        [pltpu.VMEM((GROUP, LANES), F32)],
    )(s, units, dirs, got, first)


def col_scale(pieces):
    return 1.0 / (PROTOS * (pieces[0][...] + pieces[1][...] + pieces[2][...] + pieces[3][...]))


def row_part(mass, scale, rb):
    total = jnp.zeros((LANES, LANES), F32)
    for k in range(KB):
        total = total + mass[block(rb), block(k)] * scale[k : k + 1, :]
    return rows_to_lanes(total)


def copies(out):
    value = out[0]
    for i in range(1, out.shape[0]):
        out[i] = value


def first_row_kernel(s, units, dirs, a0, a1, a2, a3, first, out, sums):
    j = pl.program_id(0)
    n = CHUNK // LANES
    rows = pl.ds(pl.multiple_of(j * n, n), n)
    scale = 1.0 / (PROTOS * (a0[rows, :] + a1[rows, :] + a2[rows, :] + a3[rows, :]))

    @pl.when(j == 0)
    def _():
        sums[...] = jnp.zeros_like(sums)

    for q in range(CHUNK // TILE):
        for rb in range(RB):
            part = mass_block(units, dirs[:, tile(q)], rb)
            total = sums[block(rb), :]
            for k in range(TILE // LANES):
                at = q * (TILE // LANES) + k
                total = total + part[:, block(k)] * scale[at : at + 1, :]
            sums[block(rb), :] = total

    @pl.when(j == pl.num_programs(0) - 1)
    def _():
        for rb in range(RB):
            out[0, rb : rb + 1, :] = rows_to_lanes(sums[block(rb), :])
        copies(out)


def first_row_sums(s, units, dirs, pieces, first):
    return chunked(
        first_row_kernel,
        WIDTH // CHUNK,
        [WHOLE, DIRS] + [WHOLE] * 4 + [ANY],
        WHOLE,
        shape((PEERS, RB, LANES)),
        [pltpu.VMEM((GROUP, LANES), F32)],
    )(s, units, dirs, *pieces, first)


def row_kernel(mass, a0, a1, a2, a3, out):
    scale = col_scale((a0, a1, a2, a3))
    for rb in range(RB):
        out[0, rb : rb + 1, :] = row_part(mass, scale, rb)
    copies(out)


def last_row_kernel(mass, a0, a1, a2, a3, exps, out):
    scale = col_scale((a0, a1, a2, a3))
    for rb in range(RB):
        out[0, rb : rb + 1, :] = row_part(mass, scale, rb)
    out[0, RB : 2 * RB, :] = exps[...]
    copies(out)


def student_kernel(s, r0, r1, r2, r3, protos, exps, hat, sums, dirs):
    j = pl.program_id(0)
    put_dirs(protos, dirs)

    @pl.when(j == 0)
    def _():
        sums[...] = jnp.zeros_like(sums)
        for b, rows in enumerate((r0, r1, r2, r3)):
            hat[own_rows(s, b), :] = unit(rows[...], 1)[0].astype(BF16)

    for q in range(CHUNK // TILE):
        for rb in range(RB):
            part = jnp.exp(dot(hat[block(rb), :], dirs[:, tile(q)]) * (1.0 / STUDENT_TEMP))
            sums[block(rb), :] = sums[block(rb), :] + fold_lanes(part)

    @pl.when(j == pl.num_programs(0) - 1)
    def _():
        for rb in range(RB):
            exps[rb : rb + 1, :] = rows_to_lanes(sums[block(rb), :])


def student_exps(s, rows, protos):
    return chunked(
        student_kernel,
        WIDTH // CHUNK,
        [ROW_BLOCK] * NY + [proto_block(CHUNK)],
        [WHOLE, WHOLE],
        [shape((RB, LANES)), shape((GROUP, DEPTH), BF16)],
        [pltpu.VMEM((GROUP, LANES), F32), pltpu.VMEM((DEPTH, CHUNK), BF16)],
    )(s, *rows, protos)


def pick_kernel(s, source, features, out):
    me = (s[0] * NY + s[1]) * NC + s[2]
    marks = lax.shift_right_logical(source[...], 8) == me
    local = jnp.bitwise_and(source[...], ROWS - 1).astype(F32)
    counts = exclusive_counts(jnp.where(marks, 1.0, 0.0))
    counts = jnp.where(marks, counts, -1.0)
    rank = lax.broadcasted_iota(jnp.int32, (PARTS, SLOT, ROWS), 1).astype(F32)
    shown = jnp.where(counts[:, None, :] == rank, local[:, None, :], 0.0)
    asked = jnp.sum(shown, axis=2, keepdims=True)
    lane = lax.broadcasted_iota(jnp.int32, (PARTS, SLOT, ROWS), 2).astype(F32)
    pick = jnp.where(asked == lane, 1.0, 0.0).reshape(ROWS, ROWS).astype(BF16)
    rows = dot(pick, features[...])
    for x in range(NX):
        for c in range(NC):
            parts = []
            for y in range(NY):
                e = ((x * NY + y) * NC + c) * SLOT
                parts.append(rows[e : e + SLOT, :])
            parcel = jnp.concatenate(parts, axis=0).astype(BF16)
            for y in range(NY):
                out[(x * NY + y) * NC + c] = parcel


def pick_rows(s, source, features):
    return pl.pallas_call(
        pick_kernel,
        in_specs=[pl.BlockSpec(memory_space=pltpu.SMEM), WHOLE, WHOLE],
        out_specs=WHOLE,
        out_shape=shape((PARTS, NY * SLOT, DEPTH), BF16),
        cost_estimate=COST,
        compiler_params=PARAMS,
    )(s, source, features)


def matched_kernel(s, source, arrived, dirs, mass, units):
    j = pl.program_id(0)

    @pl.when(j == 0)
    def _():
        index = lax.broadcasted_iota(jnp.int32, (PARTS, ROWS), 0)
        part = lax.broadcasted_iota(jnp.int32, (PARTS, ROWS), 0)
        slot = lax.broadcasted_iota(jnp.int32, (ROWS, ROWS), 0).astype(F32)
        rows = arrived[...].astype(F32)
        for y in range(NY):
            e = (s[0] * NY + y) * NC + s[2]
            mine = jnp.sum(jnp.where(index == e, source[...], 0), axis=0, keepdims=True)
            owner = lax.shift_right_logical(mine, 8)
            marks = jnp.where(part == owner, 1.0, 0.0)
            rank = jnp.sum(marks * exclusive_counts(marks), axis=0, keepdims=True)
            place = jnp.where(slot == owner.astype(F32) * SLOT + rank, 1.0, 0.0).astype(BF16)
            came = rows[:, y * SLOT : (y + 1) * SLOT, :].reshape(ROWS, DEPTH).astype(BF16)
            matched = lax.dot_general(place, came, (((0,), (0,)), ((), ())), preferred_element_type=F32)
            units[y * ROWS : (y + 1) * ROWS, :] = unit(matched, 1)[0].astype(BF16)

    for q in range(CHUNK // TILE):
        for rb in range(RB):
            mass[block(rb), tile_at(j, q)] = mass_block(units, dirs[:, tile(q)], rb)


def matched_mass(s, source, arrived, dirs):
    return chunked(
        matched_kernel,
        WIDTH // CHUNK,
        [WHOLE, WHOLE, DIRS],
        [WHOLE, WHOLE],
        [shape((GROUP, WIDTH)), shape((GROUP, DEPTH), BF16)],
    )(s, source, arrived, dirs)


def target_kernel(s, mass, a0, a1, a2, a3, got, hat, protos, targets, exps, out, sums, cross, dirs):
    j = pl.program_id(0)
    n = CHUNK // LANES

    @pl.when(j == 0)
    def _():
        sums[...] = jnp.zeros_like(sums)
        cross[...] = jnp.zeros_like(cross)
        exps[...] = jnp.sum(got[...], axis=0)

    put_dirs(protos, dirs)
    rows = pl.ds(pl.multiple_of(j * n, n), n)
    scale = (CROPS / PROTOS) / (a0[rows, :] + a1[rows, :] + a2[rows, :] + a3[rows, :])
    row_scale = 1.0 / (CROPS * exps[:RB, :])
    for rb in range(RB):
        factor = lanes_to_rows(row_scale[rb : rb + 1, :])
        scores = dot(hat[block(rb), :], dirs[...]) * (1.0 / STUDENT_TEMP)
        total = jnp.zeros((LANES, LANES), F32)
        crossed = jnp.zeros((LANES, LANES), F32)
        for k in range(n):
            cols = pl.ds(pl.multiple_of(j * CHUNK + k * LANES, LANES), LANES)
            value = (mass[block(rb), cols] * factor * scale[k : k + 1, :]).astype(BF16)
            targets[block(rb), block(k)] = value
            value = value.astype(F32)
            total = total + value
            crossed = crossed + value * scores[:, block(k)]
        sums[block(rb), :] = sums[block(rb), :] + total
        cross[...] = cross[...] + crossed

    @pl.when(j == pl.num_programs(0) - 1)
    def _():
        loss = jnp.zeros((1, LANES), F32)
        for rb in range(RB):
            total = rows_to_lanes(sums[block(rb), :])
            out[0, rb : rb + 1, :] = total
            loss = loss + total * jnp.log(exps[RB + rb : RB + rb + 1, :])
        loss = loss - jnp.sum(cross[...], axis=0, keepdims=True)
        out[0, RB : 2 * RB, :] = jnp.broadcast_to(loss, (RB, LANES))
        copies(out)


def make_targets(s, mass, pieces, got, hat, protos):
    return chunked(
        target_kernel,
        WIDTH // CHUNK,
        [WHOLE] * 7 + [proto_block(CHUNK)],
        [GROUP_ROWS, WHOLE, WHOLE],
        [
            shape((GROUP, WIDTH), BF16),
            shape((2 * RB, LANES)),
            shape((PEERS, 2 * RB, LANES)),
        ],
        [
            pltpu.VMEM((GROUP, LANES), F32),
            pltpu.VMEM((LANES, LANES), F32),
            pltpu.VMEM((DEPTH, CHUNK), BF16),
        ],
    )(s, mass, *pieces, got, hat, protos)


def grad_kernel(
    s, targets, exps, got, hat, protos, r0, r1, r2, r3, f0, f1, f2, f3, keep, give, loss,
    factor, grads, turned, dirs, feature
):
    j = pl.program_id(0)

    @pl.when(j == 0)
    def _():
        totals = jnp.sum(got[...], axis=0)
        loss[...] = totals[RB:, :]
        scale = totals[:RB, :] / exps[RB:, :]
        for rb in range(RB):
            factor[block(rb), :] = lanes_to_rows(scale[rb : rb + 1, :])
        turned[...] = hat[...].astype(F32).T.astype(BF16)
        feature[...] = jnp.zeros_like(feature)

    put_dirs(protos, dirs)
    for rb in range(RB):
        probs = jnp.exp(dot(hat[block(rb), :], dirs[...]) * (1.0 / STUDENT_TEMP))
        for k in range(GRAD_CHUNK // LANES):
            came = targets[block(rb), block(k)].astype(F32)
            value = probs[:, block(k)] * factor[block(rb), :] - came
            grads[block(rb), block(k)] = (value * (1.0 / STUDENT_TEMP)).astype(BF16)
    feature[...] = feature[...] + lax.dot_general(
        grads[...], dirs[...], (((1,), (1,)), ((), ())), preferred_element_type=F32
    )
    weights = dot(turned[...], grads[...])
    for k in range(GRAD_CHUNK // LANES):
        weight = weights[:, block(k)]
        floats, inverse = unit(protos[:, block(k)], 0)
        stat = jnp.sum(weight * dirs[:, block(k)].astype(F32), axis=0, keepdims=True)
        weight = ((weight - floats * stat) * inverse).reshape(NX * NY, NC, DEPTH // PARTS, LANES)
        own = s[2] == 0
        keep[:, :, block(k)] = jnp.where(own, weight[:, 0], weight[:, 1])
        give[:, :, block(k)] = jnp.where(own, weight[:, 1], weight[:, 0])

    @pl.when(j == pl.num_programs(0) - 1)
    def _():
        for b, (rows, out) in enumerate(((r0, f0), (r1, f1), (r2, f2), (r3, f3))):
            units, inverse = unit(rows[...], 1)
            value = feature[own_rows(s, b), :]
            along = jnp.sum(units * value, axis=1, keepdims=True)
            out[...] = (value - units * along) * inverse


def gradients(s, targets, exps, got, hat, protos, rows):
    share = (NX * NY, DEPTH // PARTS, WIDTH)
    part = pl.BlockSpec((NX * NY, DEPTH // PARTS, GRAD_CHUNK), lambda j, s: (0, 0, j))
    columns = pl.BlockSpec((GROUP, GRAD_CHUNK), lambda j, s: (0, j))
    return chunked(
        grad_kernel,
        WIDTH // GRAD_CHUNK,
        [columns, WHOLE, WHOLE, WHOLE, proto_block(GRAD_CHUNK)] + [ROW_BLOCK] * NY,
        [WHOLE] * NY + [part, part, WHOLE],
        [shape((ROWS, DEPTH))] * NY + [shape(share), shape(share), shape((RB, LANES))],
        [
            pltpu.VMEM((GROUP, LANES), F32),
            pltpu.VMEM((GROUP, GRAD_CHUNK), BF16),
            pltpu.VMEM((DEPTH, GROUP), BF16),
            pltpu.VMEM((DEPTH, GRAD_CHUNK), BF16),
            pltpu.VMEM((GROUP, DEPTH), F32),
        ],
    )(s, targets, exps, got, hat, protos, *rows)


def add_kernel(s, a, b, first, out):
    out[...] = a[...] + b[...]


def add_shares(s, a, b, first):
    part = pl.BlockSpec((NY, DEPTH // PARTS, WIDTH), lambda j, s: (j, 0, 0))
    return chunked(add_kernel, NX, [part, part, ANY], part, shape(a.shape))(s, a, b, first)


def join_kernel(z, *args):
    out = args[-1]
    for b, piece in enumerate(args[:-1]):
        k = lax.rem(z[0] - b + NZ, NZ) * (ROWS // NZ)
        out[pl.ds(pl.multiple_of(k, ROWS // NZ), ROWS // NZ), :] = piece[...]


def join_z(z, pieces):
    return pl.pallas_call(
        join_kernel,
        in_specs=[pl.BlockSpec(memory_space=pltpu.SMEM)] + [WHOLE] * NZ,
        out_specs=WHOLE,
        out_shape=shape((ROWS, DEPTH)),
        cost_estimate=COST,
        compiler_params=PARAMS,
    )(z, *pieces)


def shift(v, axis, size, step):
    return lax.ppermute(v, axis, [(i, (i + step) % size) for i in range(size)])


def gather_y(v):
    return [v] + [shift(v, "y", NY, b) for b in range(1, NY)]


def swap_rows(v):
    return lax.all_to_all(v, ("y", "z"), 0, 0, tiled=True)


def column_pieces(v):
    v = v + shift(v, "c", NC, 1)
    return [v] + [shift(v, "x", NX, b) for b in range(1, NX)]


def body(teacher_features, teacher_protos, student_features, student_protos, student_source):
    s = jnp.stack([lax.axis_index(a) for a in DP]).astype(jnp.int32)
    teacher_protos = pltpu.with_memory_space_constraint(teacher_protos, pltpu.HBM)
    student_protos = pltpu.with_memory_space_constraint(student_protos, pltpu.HBM)
    source = lax.all_to_all(
        jnp.broadcast_to(student_source[None], (PARTS, ROWS)), DP, 0, 0, tiled=True
    )
    column, dirs, units = teacher_units(s, gather_y(teacher_features), teacher_protos)
    got = swap_rows(first_row_sums(s, units, dirs, column_pieces(column), source))

    student_rows = gather_y(student_features)
    exps, hat = student_exps(s, student_rows, student_protos)
    mass, column = columns_again(s, units, dirs, got, exps, 1)
    parts = call(row_kernel, shape((PEERS, RB, LANES)), mass, *column_pieces(column))
    got = swap_rows(parts)

    parcel = pick_rows(s, source, teacher_features)
    arrived = lax.all_to_all(parcel, DP, 0, 0, tiled=True)
    (column,) = columns_again(s, units, dirs, got, exps, 0)
    mass, _ = matched_mass(s, source, arrived, dirs)
    pieces = column_pieces(column)
    got = swap_rows(call(last_row_kernel, shape((PEERS, 2 * RB, LANES)), mass, *pieces, exps))

    targets, exps, parts = make_targets(s, mass, pieces, got, hat, student_protos)
    got = swap_rows(parts)
    *features, keep, give, loss = gradients(
        s, targets, exps, got, hat, student_protos, student_rows
    )
    feature = features[0]
    for b in range(1, NY):
        feature = feature + shift(features[b], "y", NY, NY - b)
    feature = lax.all_to_all(feature.reshape(NZ, ROWS // NZ, DEPTH), "z", 0, 0, tiled=True)
    feature = jnp.sum(feature, axis=0)
    loss = functools.reduce(jnp.add, column_pieces(loss))
    weight = add_shares(s, keep, shift(give, "c", NC, 1), loss)
    weight = lax.all_to_all(weight, ("x", "y"), 0, 0, tiled=True)

    z = lax.axis_index("z").astype(jnp.int32).reshape(1)
    pieces = [feature] + [shift(feature, "z", NZ, b) for b in range(1, NZ)]
    grad_features = join_z(z, pieces)

    weight = jnp.sum(weight.reshape(NX, NY, DEPTH // PARTS, WIDTH), axis=0)
    grad_protos = weight.transpose(1, 0, 2).reshape(DEPTH // PARTS, NY * WIDTH)

    loss = jnp.sum(loss[0]) / CROPS
    return (loss, grad_features, grad_protos)


def solution(mesh):
    return jax.shard_map(
        body,
        mesh=Mesh(mesh.devices.reshape(NX, NY, NC, NZ), ("x", "y", "c", "z")),
        in_specs=(P(DP, None), P(None, "z"), P(DP, None), P(None, "z"), P(DP)),
        out_specs=(P(), P(DP, None), P(DP, "z")),
        check_vma=False,
    )
```

```python
import functools

import jax
import jax.numpy as jnp
from jax import lax
from jax.experimental import pallas as pl
from jax.experimental.pallas import tpu as pltpu
from jax.sharding import Mesh, PartitionSpec as P

PROTOS = 65536
CROPS = 8192
ITERS = 3
NX, NY, NC, NZ = 4, 4, 2, 8
DP = ("x", "y", "c")
PARTS = NX * NY * NC
ROWS = CROPS // PARTS
SLOT = ROWS // PARTS
DEPTH = 256
GROUP = NY * ROWS
WIDTH = PROTOS // (NY * NZ)
SPAN = PROTOS // NZ
CHUNK = 1024
GRAD_CHUNK = 512
LANES = 128
TILE = 256
RB = GROUP // LANES
KB = WIDTH // LANES
OWN = ROWS // LANES
PEERS = NY * NZ

TEACHER_TEMP = 0.04
STUDENT_TEMP = 0.1
NORM_EPSILON = 1e-06
F32 = jnp.float32
BF16 = jnp.bfloat16

WHOLE = pl.BlockSpec(memory_space=pltpu.VMEM)
PARAMS = pltpu.CompilerParams(vmem_limit_bytes=30 << 20)
COST = pl.CostEstimate(flops=0, bytes_accessed=36000, transcendentals=0)
ROW_BLOCK = pl.BlockSpec((ROWS, DEPTH), lambda j, s: (0, 0))


def proto_block(chunk):
    return split_rows(DEPTH, chunk, 4, lambda j, s: s[1] * (WIDTH // chunk) + j)


def call(kernel, out_shape, *args):
    return pl.pallas_call(
        kernel,
        in_specs=[WHOLE] * len(args),
        out_specs=jax.tree.map(lambda _: WHOLE, out_shape),
        out_shape=out_shape,
        cost_estimate=COST,
        compiler_params=PARAMS,
    )(*args)


class Joined:
    def __init__(self, refs):
        self.refs = refs

    @property
    def shape(self):
        return (sum(r.shape[0] for r in self.refs), self.refs[0].shape[1])

    def __getitem__(self, at):
        return jnp.concatenate([r[at] for r in self.refs], axis=0)


def split_rows(rows, columns, parts, place):
    def spec(r):
        return pl.BlockSpec((rows // parts, columns), lambda j, s: (r, place(j, s)))

    return [spec(r) for r in range(parts)]


def chunked(kernel, steps, in_specs, out_specs, out_shape, scratch=()):
    groups = [spec if isinstance(spec, list) else [spec] for spec in in_specs]

    def regrouped(s, *refs):
        refs, args = list(refs), []
        for spec, group in zip(in_specs, groups):
            mine, refs = refs[: len(group)], refs[len(group) :]
            args.append(Joined(mine) if isinstance(spec, list) else mine[0])
        return kernel(s, *args, *refs)

    run = pl.pallas_call(
        regrouped,
        grid_spec=pltpu.PrefetchScalarGridSpec(
            num_scalar_prefetch=1,
            grid=(steps,),
            in_specs=[spec for group in groups for spec in group],
            out_specs=out_specs,
            scratch_shapes=scratch,
        ),
        out_shape=out_shape,
        cost_estimate=COST,
        compiler_params=PARAMS,
    )

    def apply(s, *args):
        return run(s, *[a for a, group in zip(args, groups, strict=True) for _ in group])

    return apply


def shape(dims, dtype=F32):
    return jax.ShapeDtypeStruct(dims, dtype)


def far(dims, dtype=F32):
    return pltpu.HBM(dims, dtype)


def hbm(v):
    return pltpu.with_memory_space_constraint(v, pltpu.HBM)


def unit(values, axis):
    floats = values.astype(F32)
    inverse = 1.0 / jnp.sqrt(jnp.sum(floats * floats, axis=axis, keepdims=True) + NORM_EPSILON)
    return floats * inverse, inverse


def own_rows(s, b):
    return pl.ds(pl.multiple_of(lax.rem(s[1] - b + NY, NY) * ROWS, ROWS), ROWS)


def block(rb):
    return slice(rb * LANES, (rb + 1) * LANES)


def tile(q):
    return slice(q * TILE, (q + 1) * TILE)


def tile_at(j, q):
    return pl.ds(pl.multiple_of(j * CHUNK + q * TILE, TILE), TILE)


def put_dirs(protos, dirs):
    width = protos.shape[1]
    sums = []
    for k in range(width // LANES):
        floats = protos[:, block(k)].astype(F32)
        parts = (floats * floats).reshape(4, DEPTH // 32, 8, LANES)
        sums.append(jnp.sum(jnp.sum(parts, axis=1), axis=0))
    total = jnp.sum(jnp.concatenate(sums, axis=1), axis=0, keepdims=True)
    inverse = 1.0 / jnp.sqrt(total + NORM_EPSILON)
    for k in range(width // LANES):
        dirs[:, block(k)] = (protos[:, block(k)].astype(F32) * inverse[:, block(k)]).astype(BF16)


def lanes_to_rows(row):
    return jnp.broadcast_to(row, (LANES, LANES)).T


def fold_lanes(values):
    return functools.reduce(jnp.add, [values[:, block(k)] for k in range(values.shape[1] // LANES)])


def rows_to_lanes(values):
    return jnp.sum(values.T, axis=0, keepdims=True)


def dot(a, b):
    return jnp.dot(a, b, preferred_element_type=F32)


def exclusive_counts(marks):
    n = marks.shape[1]
    before = lax.broadcasted_iota(jnp.int32, (n, n), 0) < lax.broadcasted_iota(jnp.int32, (n, n), 1)
    return dot(marks.astype(BF16), before.astype(BF16))


def mass_block(units, dirs, rb):
    return jnp.exp(dot(units[block(rb), :], dirs) * (1.0 / TEACHER_TEMP))


def put_column(column, q, total):
    total = jnp.sum(total, axis=0, keepdims=True)
    for k in range(TILE // LANES):
        row = q * (TILE // LANES) + k
        column[row : row + 1, :] = total[:, block(k)]


def add_rows(total, part):
    return total + jnp.sum(part.reshape(LANES // 8, 8, TILE), axis=0)


def mass_kernel(s, r0, r1, r2, r3, protos, column, dirs, units):
    j = pl.program_id(0)

    @pl.when(j == 0)
    def _():
        for b, rows in enumerate((r0, r1, r2, r3)):
            units[own_rows(s, b), :] = unit(rows[...], 1)[0].astype(BF16)

    put_dirs(protos, dirs)
    for q in range(CHUNK // TILE):
        total = jnp.zeros((8, TILE), F32)
        for rb in range(RB):
            total = add_rows(total, mass_block(units, dirs[:, tile(q)], rb))
        put_column(column, q, total)


COLUMN = pl.BlockSpec((CHUNK // LANES, LANES), lambda j, s: (j, 0))
DIRS_OUT = pl.BlockSpec((DEPTH, CHUNK), lambda j, s: (0, j))
DIRS = split_rows(DEPTH, CHUNK, 4, lambda j, s: j)
ANY = pl.BlockSpec(memory_space=pl.ANY)
GROUP_ROWS = pl.BlockSpec((GROUP, CHUNK), lambda j, s: (0, j))


def teacher_units(s, rows, protos):
    return chunked(
        mass_kernel,
        WIDTH // CHUNK,
        [ROW_BLOCK] * NY + [proto_block(CHUNK)],
        [COLUMN, DIRS_OUT, WHOLE],
        [
            shape((KB, LANES)),
            shape((DEPTH, WIDTH), BF16),
            shape((GROUP, DEPTH), BF16),
        ],
    )(s, *rows, protos)


def again_kernel(keep, s, units, dirs, got, *rest):
    j = pl.program_id(0)
    outs = rest[-3 if keep else -2 :]
    column, factor = outs[-2:]

    @pl.when(j == 0)
    def _():
        scale = 1.0 / (CROPS * jnp.sum(got[...], axis=0))
        for rb in range(RB):
            factor[block(rb), :] = lanes_to_rows(scale[rb : rb + 1, :])

    for q in range(CHUNK // TILE):
        total = jnp.zeros((8, TILE), F32)
        for rb in range(RB):
            part = mass_block(units, dirs[:, tile(q)], rb)
            if len(outs) == 3:
                outs[0][block(rb), tile_at(j, q)] = part
            scaled = [part[:, block(k)] * factor[block(rb), :] for k in range(TILE // LANES)]
            total = add_rows(total, jnp.concatenate(scaled, axis=1))
        put_column(column, q, total)


def columns_again(s, units, dirs, got, first, keep):
    return chunked(
        functools.partial(again_kernel, keep),
        WIDTH // CHUNK,
        [WHOLE, DIRS, WHOLE] + [ANY] * len(first),
        [WHOLE] * keep + [COLUMN],
        [shape((GROUP, WIDTH))] * keep + [shape((KB, LANES))],
        [pltpu.VMEM((GROUP, LANES), F32)],
    )(s, units, dirs, got, *first)


def col_scale(pieces):
    return 1.0 / (PROTOS * (pieces[0][...] + pieces[1][...] + pieces[2][...] + pieces[3][...]))


def row_part(mass, scale, rb):
    total = jnp.zeros((LANES, LANES), F32)
    for k in range(KB):
        total = total + mass[block(rb), block(k)] * scale[k : k + 1, :]
    return rows_to_lanes(total)


def copies(out):
    value = out[0]
    for i in range(1, out.shape[0]):
        out[i] = value


def first_row_kernel(s, units, dirs, a0, a1, a2, a3, first, out, sums):
    j = pl.program_id(0)
    n = CHUNK // LANES
    rows = pl.ds(pl.multiple_of(j * n, n), n)
    scale = 1.0 / (PROTOS * (a0[rows, :] + a1[rows, :] + a2[rows, :] + a3[rows, :]))

    @pl.when(j == 0)
    def _():
        sums[...] = jnp.zeros_like(sums)

    for q in range(CHUNK // TILE):
        for rb in range(RB):
            part = mass_block(units, dirs[:, tile(q)], rb)
            total = sums[block(rb), :]
            for k in range(TILE // LANES):
                at = q * (TILE // LANES) + k
                total = total + part[:, block(k)] * scale[at : at + 1, :]
            sums[block(rb), :] = total

    @pl.when(j == pl.num_programs(0) - 1)
    def _():
        for rb in range(RB):
            out[0, rb : rb + 1, :] = rows_to_lanes(sums[block(rb), :])
        copies(out)


def first_row_sums(s, units, dirs, pieces, first):
    return chunked(
        first_row_kernel,
        WIDTH // CHUNK,
        [WHOLE, DIRS] + [WHOLE] * 4 + [ANY],
        WHOLE,
        shape((PEERS, RB, LANES)),
        [pltpu.VMEM((GROUP, LANES), F32)],
    )(s, units, dirs, *pieces, first)


def row_kernel(mass, a0, a1, a2, a3, out):
    scale = col_scale((a0, a1, a2, a3))
    for rb in range(RB):
        out[0, rb : rb + 1, :] = row_part(mass, scale, rb)
    copies(out)


def last_row_kernel(mass, a0, a1, a2, a3, exps, out):
    scale = col_scale((a0, a1, a2, a3))
    for rb in range(RB):
        out[0, rb : rb + 1, :] = row_part(mass, scale, rb)
    out[0, RB : 2 * RB, :] = exps[...]
    copies(out)


def student_kernel(s, r0, r1, r2, r3, protos, exps, hat, sums, dirs):
    j = pl.program_id(0)
    put_dirs(protos, dirs)

    @pl.when(j == 0)
    def _():
        sums[...] = jnp.zeros_like(sums)
        for b, rows in enumerate((r0, r1, r2, r3)):
            hat[own_rows(s, b), :] = unit(rows[...], 1)[0].astype(BF16)

    for q in range(CHUNK // TILE):
        for rb in range(RB):
            part = jnp.exp(dot(hat[block(rb), :], dirs[:, tile(q)]) * (1.0 / STUDENT_TEMP))
            sums[block(rb), :] = sums[block(rb), :] + fold_lanes(part)

    @pl.when(j == pl.num_programs(0) - 1)
    def _():
        for rb in range(RB):
            exps[rb : rb + 1, :] = rows_to_lanes(sums[block(rb), :])


def student_exps(s, rows, protos):
    return chunked(
        student_kernel,
        WIDTH // CHUNK,
        [ROW_BLOCK] * NY + [proto_block(CHUNK)],
        [WHOLE, WHOLE],
        [shape((RB, LANES)), shape((GROUP, DEPTH), BF16)],
        [pltpu.VMEM((GROUP, LANES), F32), pltpu.VMEM((DEPTH, CHUNK), BF16)],
    )(s, *rows, protos)


def pick_kernel(s, source, features, first, out):
    me = (s[0] * NY + s[1]) * NC + s[2]
    marks = lax.shift_right_logical(source[...], 8) == me
    local = jnp.bitwise_and(source[...], ROWS - 1).astype(F32)
    counts = exclusive_counts(jnp.where(marks, 1.0, 0.0))
    counts = jnp.where(marks, counts, -1.0)
    rank = lax.broadcasted_iota(jnp.int32, (PARTS, SLOT, ROWS), 1).astype(F32)
    shown = jnp.where(counts[:, None, :] == rank, local[:, None, :], 0.0)
    asked = jnp.sum(shown, axis=2, keepdims=True)
    lane = lax.broadcasted_iota(jnp.int32, (PARTS, SLOT, ROWS), 2).astype(F32)
    pick = jnp.where(asked == lane, 1.0, 0.0).reshape(ROWS, ROWS).astype(BF16)
    rows = dot(pick, features[...])
    for x in range(NX):
        for c in range(NC):
            parts = []
            for y in range(NY):
                e = ((x * NY + y) * NC + c) * SLOT
                parts.append(rows[e : e + SLOT, :])
            parcel = jnp.concatenate(parts, axis=0).astype(BF16)
            for y in range(NY):
                out[(x * NY + y) * NC + c] = parcel


def pick_rows(s, source, features, first):
    return pl.pallas_call(
        pick_kernel,
        in_specs=[pl.BlockSpec(memory_space=pltpu.SMEM), WHOLE, WHOLE, ANY],
        out_specs=WHOLE,
        out_shape=shape((PARTS, NY * SLOT, DEPTH), BF16),
        cost_estimate=COST,
        compiler_params=PARAMS,
    )(s, source, features, first)


def matched_kernel(s, source, arrived, dirs, mass, units):
    j = pl.program_id(0)

    @pl.when(j == 0)
    def _():
        index = lax.broadcasted_iota(jnp.int32, (PARTS, ROWS), 0)
        part = lax.broadcasted_iota(jnp.int32, (PARTS, ROWS), 0)
        slot = lax.broadcasted_iota(jnp.int32, (ROWS, ROWS), 0).astype(F32)
        rows = arrived[...].astype(F32)
        for y in range(NY):
            e = (s[0] * NY + y) * NC + s[2]
            mine = jnp.sum(jnp.where(index == e, source[...], 0), axis=0, keepdims=True)
            owner = lax.shift_right_logical(mine, 8)
            marks = jnp.where(part == owner, 1.0, 0.0)
            rank = jnp.sum(marks * exclusive_counts(marks), axis=0, keepdims=True)
            place = jnp.where(slot == owner.astype(F32) * SLOT + rank, 1.0, 0.0).astype(BF16)
            came = rows[:, y * SLOT : (y + 1) * SLOT, :].reshape(ROWS, DEPTH).astype(BF16)
            matched = lax.dot_general(place, came, (((0,), (0,)), ((), ())), preferred_element_type=F32)
            units[y * ROWS : (y + 1) * ROWS, :] = unit(matched, 1)[0].astype(BF16)

    for q in range(CHUNK // TILE):
        for rb in range(RB):
            mass[block(rb), tile_at(j, q)] = mass_block(units, dirs[:, tile(q)], rb)


def matched_mass(s, source, arrived, dirs):
    return chunked(
        matched_kernel,
        WIDTH // CHUNK,
        [WHOLE, WHOLE, DIRS],
        [WHOLE, WHOLE],
        [shape((GROUP, WIDTH)), shape((GROUP, DEPTH), BF16)],
    )(s, source, arrived, dirs)


def target_kernel(s, mass, a0, a1, a2, a3, got, hat, protos, targets, exps, out, sums, cross, dirs):
    j = pl.program_id(0)
    n = CHUNK // LANES

    @pl.when(j == 0)
    def _():
        sums[...] = jnp.zeros_like(sums)
        cross[...] = jnp.zeros_like(cross)
        exps[...] = jnp.sum(got[...], axis=0)

    put_dirs(protos, dirs)
    rows = pl.ds(pl.multiple_of(j * n, n), n)
    scale = (CROPS / PROTOS) / (a0[rows, :] + a1[rows, :] + a2[rows, :] + a3[rows, :])
    row_scale = 1.0 / (CROPS * exps[:RB, :])
    for rb in range(RB):
        factor = lanes_to_rows(row_scale[rb : rb + 1, :])
        scores = dot(hat[block(rb), :], dirs[...]) * (1.0 / STUDENT_TEMP)
        total = jnp.zeros((LANES, LANES), F32)
        crossed = jnp.zeros((LANES, LANES), F32)
        for k in range(n):
            cols = pl.ds(pl.multiple_of(j * CHUNK + k * LANES, LANES), LANES)
            value = (mass[block(rb), cols] * factor * scale[k : k + 1, :]).astype(BF16)
            targets[block(rb), cols] = value
            value = value.astype(F32)
            total = total + value
            crossed = crossed + value * scores[:, block(k)]
        sums[block(rb), :] = sums[block(rb), :] + total
        cross[...] = cross[...] + crossed

    @pl.when(j == pl.num_programs(0) - 1)
    def _():
        loss = jnp.zeros((1, LANES), F32)
        for rb in range(RB):
            total = rows_to_lanes(sums[block(rb), :])
            out[0, rb : rb + 1, :] = total
            loss = loss + total * jnp.log(exps[RB + rb : RB + rb + 1, :])
        loss = loss - jnp.sum(cross[...], axis=0, keepdims=True)
        out[0, RB : 2 * RB, :] = jnp.broadcast_to(loss, (RB, LANES))
        copies(out)


def make_targets(s, mass, pieces, got, hat, protos):
    return chunked(
        target_kernel,
        WIDTH // CHUNK,
        [WHOLE] * 7 + [proto_block(CHUNK)],
        [WHOLE, WHOLE, WHOLE],
        [
            shape((GROUP, WIDTH), BF16),
            shape((2 * RB, LANES)),
            shape((PEERS, 2 * RB, LANES)),
        ],
        [
            pltpu.VMEM((GROUP, LANES), F32),
            pltpu.VMEM((LANES, LANES), F32),
            pltpu.VMEM((DEPTH, CHUNK), BF16),
        ],
    )(s, mass, *pieces, got, hat, protos)


def grad_kernel(
    s, targets, exps, got, hat, protos, r0, r1, r2, r3, f0, f1, f2, f3, keep, give, loss,
    factor, grads, turned, dirs, feature
):
    j = pl.program_id(0)

    @pl.when(j == 0)
    def _():
        totals = jnp.sum(got[...], axis=0)
        loss[...] = totals[RB:, :]
        scale = totals[:RB, :] / exps[RB:, :]
        for rb in range(RB):
            factor[block(rb), :] = lanes_to_rows(scale[rb : rb + 1, :])
        turned[...] = hat[...].astype(F32).T.astype(BF16)
        feature[...] = jnp.zeros_like(feature)

    put_dirs(protos, dirs)
    for rb in range(RB):
        probs = jnp.exp(dot(hat[block(rb), :], dirs[...]) * (1.0 / STUDENT_TEMP))
        for k in range(GRAD_CHUNK // LANES):
            cols = pl.ds(pl.multiple_of(j * GRAD_CHUNK + k * LANES, LANES), LANES)
            came = targets[block(rb), cols].astype(F32)
            value = probs[:, block(k)] * factor[block(rb), :] - came
            grads[block(rb), block(k)] = (value * (1.0 / STUDENT_TEMP)).astype(BF16)
    feature[...] = feature[...] + lax.dot_general(
        grads[...], dirs[...], (((1,), (1,)), ((), ())), preferred_element_type=F32
    )
    weights = dot(turned[...], grads[...])
    for k in range(GRAD_CHUNK // LANES):
        weight = weights[:, block(k)]
        floats, inverse = unit(protos[:, block(k)], 0)
        stat = jnp.sum(weight * dirs[:, block(k)].astype(F32), axis=0, keepdims=True)
        weight = ((weight - floats * stat) * inverse).reshape(NX * NY, NC, DEPTH // PARTS, LANES)
        own = s[2] == 0
        keep[:, :, block(k)] = jnp.where(own, weight[:, 0], weight[:, 1])
        give[:, :, block(k)] = jnp.where(own, weight[:, 1], weight[:, 0])

    @pl.when(j == pl.num_programs(0) - 1)
    def _():
        for b, (rows, out) in enumerate(((r0, f0), (r1, f1), (r2, f2), (r3, f3))):
            units, inverse = unit(rows[...], 1)
            value = feature[own_rows(s, b), :]
            along = jnp.sum(units * value, axis=1, keepdims=True)
            out[...] = (value - units * along) * inverse


def gradients(s, targets, exps, got, hat, protos, rows):
    share = (NX * NY, DEPTH // PARTS, WIDTH)
    part = pl.BlockSpec((NX * NY, DEPTH // PARTS, GRAD_CHUNK), lambda j, s: (0, 0, j))
    return chunked(
        grad_kernel,
        WIDTH // GRAD_CHUNK,
        [WHOLE, WHOLE, WHOLE, WHOLE, proto_block(GRAD_CHUNK)] + [ROW_BLOCK] * NY,
        [WHOLE] * NY + [part, part, WHOLE],
        [shape((ROWS, DEPTH))] * NY + [shape(share), shape(share), shape((RB, LANES))],
        [
            pltpu.VMEM((GROUP, LANES), F32),
            pltpu.VMEM((GROUP, GRAD_CHUNK), BF16),
            pltpu.VMEM((DEPTH, GROUP), BF16),
            pltpu.VMEM((DEPTH, GRAD_CHUNK), BF16),
            pltpu.VMEM((GROUP, DEPTH), F32),
        ],
    )(s, targets, exps, got, hat, protos, *rows)


def add_kernel(s, a, b, first, out):
    out[...] = a[...] + b[...]


def add_shares(s, a, b, first):
    part = pl.BlockSpec((NY, DEPTH // PARTS, WIDTH), lambda j, s: (j, 0, 0))
    return chunked(add_kernel, NX, [part, part, ANY], part, shape(a.shape))(s, a, b, first)


def join_kernel(z, *args):
    out = args[-1]
    rows = args[0].shape[0]
    for b, piece in enumerate(args[:-1]):
        k = lax.rem(z[0] // 2 - b + NZ // 2, NZ // 2) * rows
        out[pl.ds(pl.multiple_of(k, rows), rows), :] = piece[...]


def join_z(z, pieces):
    return pl.pallas_call(
        join_kernel,
        in_specs=[pl.BlockSpec(memory_space=pltpu.SMEM)] + [WHOLE] * len(pieces),
        out_specs=WHOLE,
        out_shape=shape((ROWS, DEPTH)),
        cost_estimate=COST,
        compiler_params=PARAMS,
    )(z, *pieces)


def shift(v, axis, size, step):
    return lax.ppermute(v, axis, [(i, (i + step) % size) for i in range(size)])


def gather_y(v):
    return [v] + [shift(v, "y", NY, b) for b in range(1, NY)]


def swap_rows(v):
    return lax.all_to_all(v, ("y", "z"), 0, 0, tiled=True)


def column_pieces(v):
    v = v + shift(v, "c", NC, 1)
    return [v] + [shift(v, "x", NX, b) for b in range(1, NX)]


def body(teacher_features, teacher_protos, student_features, student_protos, student_source):
    s = jnp.stack([lax.axis_index(a) for a in DP]).astype(jnp.int32)
    teacher_protos = pltpu.with_memory_space_constraint(teacher_protos, pltpu.HBM)
    student_protos = pltpu.with_memory_space_constraint(student_protos, pltpu.HBM)
    source = lax.all_to_all(
        jnp.broadcast_to(student_source[None], (PARTS, ROWS)), DP, 0, 0, tiled=True
    )
    column, dirs, units = teacher_units(s, gather_y(teacher_features), teacher_protos)
    got = swap_rows(first_row_sums(s, units, dirs, column_pieces(column), source))

    student_rows = gather_y(student_features)
    exps, hat = student_exps(s, student_rows, student_protos)
    mass, column = columns_again(s, units, dirs, got, student_rows[1:], 1)
    parts = call(row_kernel, shape((PEERS, RB, LANES)), mass, *column_pieces(column))
    got = swap_rows(parts)

    parcel = pick_rows(s, source, teacher_features, exps)
    arrived = lax.all_to_all(parcel, DP, 0, 0, tiled=True)
    (column,) = columns_again(s, units, dirs, got, [exps], 0)
    mass, _ = matched_mass(s, source, arrived, dirs)
    pieces = column_pieces(column)
    got = swap_rows(call(last_row_kernel, shape((PEERS, 2 * RB, LANES)), mass, *pieces, exps))

    targets, exps, parts = make_targets(s, mass, pieces, got, hat, student_protos)
    got = swap_rows(parts)
    *features, keep, give, loss = gradients(
        s, targets, exps, got, hat, student_protos, student_rows
    )
    feature = features[0]
    for b in range(1, NY):
        feature = feature + shift(features[b], "y", NY, NY - b)
    feature = lax.all_to_all(feature.reshape(NZ, ROWS // NZ, DEPTH), "z", 0, 0, tiled=True)
    feature = jnp.sum(feature, axis=0)
    loss = functools.reduce(jnp.add, column_pieces(loss))
    weight = add_shares(s, keep, shift(give, "c", NC, 1), loss)
    weight = lax.all_to_all(weight, ("x", "y"), 0, 0, tiled=True)

    z = lax.axis_index("z").astype(jnp.int32).reshape(1)
    other = lax.ppermute(feature, "z", [(i, i ^ 1) for i in range(NZ)])
    even = z[0] % 2 == 0
    pair = jnp.concatenate([jnp.where(even, feature, other), jnp.where(even, other, feature)])
    pieces = [pair] + [shift(pair, "z", NZ, 2 * b) for b in range(1, NZ // 2)]
    grad_features = join_z(z, pieces)

    weight = jnp.sum(weight.reshape(NX, NY, DEPTH // PARTS, WIDTH), axis=0)
    grad_protos = weight.transpose(1, 0, 2).reshape(DEPTH // PARTS, NY * WIDTH)

    loss = jnp.sum(loss[0]) / CROPS
    return (loss, grad_features, grad_protos)


def solution(mesh):
    return jax.shard_map(
        body,
        mesh=Mesh(mesh.devices.reshape(NX, NY, NC, NZ), ("x", "y", "c", "z")),
        in_specs=(P(DP, None), P(None, "z"), P(DP, None), P(None, "z"), P(DP)),
        out_specs=(P(), P(DP, None), P(DP, "z")),
        check_vma=False,
    )
```

```python
import functools

import jax
import jax.numpy as jnp
from jax import lax
from jax.experimental import pallas as pl
from jax.experimental.pallas import tpu as pltpu
from jax.sharding import Mesh, PartitionSpec as P

PROTOS = 65536
CROPS = 8192
ITERS = 3
NX, NY, NC, NZ = 4, 4, 2, 8
DP = ("x", "y", "c")
PARTS = NX * NY * NC
ROWS = CROPS // PARTS
SLOT = ROWS // PARTS
DEPTH = 256
GROUP = NY * ROWS
WIDTH = PROTOS // (NY * NZ)
SPAN = PROTOS // NZ
CHUNK = 1024
GRAD_CHUNK = 512
LANES = 128
TILE = 256
RB = GROUP // LANES
KB = WIDTH // LANES
OWN = ROWS // LANES
PEERS = NY * NZ

TEACHER_TEMP = 0.04
STUDENT_TEMP = 0.1
NORM_EPSILON = 1e-06
F32 = jnp.float32
BF16 = jnp.bfloat16

WHOLE = pl.BlockSpec(memory_space=pltpu.VMEM)
PARAMS = pltpu.CompilerParams(vmem_limit_bytes=30 << 20)
COST = pl.CostEstimate(flops=0, bytes_accessed=36000, transcendentals=0)
ROW_BLOCK = pl.BlockSpec((ROWS, DEPTH), lambda j, s: (0, 0))


def proto_block(chunk):
    return split_rows(DEPTH, chunk, 4, lambda j, s: s[1] * (WIDTH // chunk) + j)


def call(kernel, out_shape, *args):
    return pl.pallas_call(
        kernel,
        in_specs=[WHOLE] * len(args),
        out_specs=jax.tree.map(lambda _: WHOLE, out_shape),
        out_shape=out_shape,
        cost_estimate=COST,
        compiler_params=PARAMS,
    )(*args)


class Joined:
    def __init__(self, refs):
        self.refs = refs

    @property
    def shape(self):
        return (sum(r.shape[0] for r in self.refs), self.refs[0].shape[1])

    def __getitem__(self, at):
        return jnp.concatenate([r[at] for r in self.refs], axis=0)


def split_rows(rows, columns, parts, place):
    def spec(r):
        return pl.BlockSpec((rows // parts, columns), lambda j, s: (r, place(j, s)))

    return [spec(r) for r in range(parts)]


def chunked(kernel, steps, in_specs, out_specs, out_shape, scratch=()):
    groups = [spec if isinstance(spec, list) else [spec] for spec in in_specs]

    def regrouped(s, *refs):
        refs, args = list(refs), []
        for spec, group in zip(in_specs, groups):
            mine, refs = refs[: len(group)], refs[len(group) :]
            args.append(Joined(mine) if isinstance(spec, list) else mine[0])
        return kernel(s, *args, *refs)

    run = pl.pallas_call(
        regrouped,
        grid_spec=pltpu.PrefetchScalarGridSpec(
            num_scalar_prefetch=1,
            grid=(steps,),
            in_specs=[spec for group in groups for spec in group],
            out_specs=out_specs,
            scratch_shapes=scratch,
        ),
        out_shape=out_shape,
        cost_estimate=COST,
        compiler_params=PARAMS,
    )

    def apply(s, *args):
        return run(s, *[a for a, group in zip(args, groups, strict=True) for _ in group])

    return apply


def shape(dims, dtype=F32):
    return jax.ShapeDtypeStruct(dims, dtype)


def far(dims, dtype=F32):
    return pltpu.HBM(dims, dtype)


def hbm(v):
    return pltpu.with_memory_space_constraint(v, pltpu.HBM)


def unit(values, axis):
    floats = values.astype(F32)
    inverse = 1.0 / jnp.sqrt(jnp.sum(floats * floats, axis=axis, keepdims=True) + NORM_EPSILON)
    return floats * inverse, inverse


def own_rows(s, b):
    return pl.ds(pl.multiple_of(lax.rem(s[1] - b + NY, NY) * ROWS, ROWS), ROWS)


def block(rb):
    return slice(rb * LANES, (rb + 1) * LANES)


def tile(q):
    return slice(q * TILE, (q + 1) * TILE)


def tile_at(j, q):
    return pl.ds(pl.multiple_of(j * CHUNK + q * TILE, TILE), TILE)


def put_dirs(protos, dirs):
    width = protos.shape[1]
    sums = []
    for k in range(width // LANES):
        floats = protos[:, block(k)].astype(F32)
        parts = (floats * floats).reshape(4, DEPTH // 32, 8, LANES)
        sums.append(jnp.sum(jnp.sum(parts, axis=1), axis=0))
    total = jnp.sum(jnp.concatenate(sums, axis=1), axis=0, keepdims=True)
    inverse = 1.0 / jnp.sqrt(total + NORM_EPSILON)
    for k in range(width // LANES):
        dirs[:, block(k)] = (protos[:, block(k)].astype(F32) * inverse[:, block(k)]).astype(BF16)


def lanes_to_rows(row):
    return jnp.broadcast_to(row, (LANES, LANES)).T


def fold_lanes(values):
    return functools.reduce(jnp.add, [values[:, block(k)] for k in range(values.shape[1] // LANES)])


def rows_to_lanes(values):
    return jnp.sum(values.T, axis=0, keepdims=True)


def dot(a, b):
    return jnp.dot(a, b, preferred_element_type=F32)


def exclusive_counts(marks):
    n = marks.shape[1]
    before = lax.broadcasted_iota(jnp.int32, (n, n), 0) < lax.broadcasted_iota(jnp.int32, (n, n), 1)
    return dot(marks.astype(BF16), before.astype(BF16))


def mass_block(units, dirs, rb):
    return jnp.exp(dot(units[block(rb), :], dirs) * (1.0 / TEACHER_TEMP))


def put_column(column, q, total):
    total = jnp.sum(total, axis=0, keepdims=True)
    for k in range(TILE // LANES):
        row = q * (TILE // LANES) + k
        column[row : row + 1, :] = total[:, block(k)]


def add_rows(total, part):
    return total + jnp.sum(part.reshape(LANES // 8, 8, TILE), axis=0)


def mass_kernel(s, r0, r1, r2, r3, protos, column, dirs, units):
    j = pl.program_id(0)

    @pl.when(j == 0)
    def _():
        for b, rows in enumerate((r0, r1, r2, r3)):
            units[own_rows(s, b), :] = unit(rows[...], 1)[0].astype(BF16)

    put_dirs(protos, dirs)
    for q in range(CHUNK // TILE):
        total = jnp.zeros((8, TILE), F32)
        for rb in range(RB):
            total = add_rows(total, mass_block(units, dirs[:, tile(q)], rb))
        put_column(column, q, total)


COLUMN = pl.BlockSpec((CHUNK // LANES, LANES), lambda j, s: (j, 0))
DIRS_OUT = pl.BlockSpec((DEPTH, CHUNK), lambda j, s: (0, j))
DIRS = split_rows(DEPTH, CHUNK, 4, lambda j, s: j)
ANY = pl.BlockSpec(memory_space=pl.ANY)
GROUP_ROWS = pl.BlockSpec((GROUP, CHUNK), lambda j, s: (0, j))


def teacher_units(s, rows, protos):
    return chunked(
        mass_kernel,
        WIDTH // CHUNK,
        [ROW_BLOCK] * NY + [proto_block(CHUNK)],
        [COLUMN, DIRS_OUT, WHOLE],
        [
            shape((KB, LANES)),
            shape((DEPTH, WIDTH), BF16),
            shape((GROUP, DEPTH), BF16),
        ],
    )(s, *rows, protos)


def again_kernel(keep, s, units, dirs, got, *rest):
    j = pl.program_id(0)
    outs = rest[-3 if keep else -2 :]
    column, factor = outs[-2:]

    @pl.when(j == 0)
    def _():
        scale = 1.0 / (CROPS * jnp.sum(got[...], axis=0))
        for rb in range(RB):
            factor[block(rb), :] = lanes_to_rows(scale[rb : rb + 1, :])

    for q in range(CHUNK // TILE):
        total = jnp.zeros((8, TILE), F32)
        for rb in range(RB):
            part = mass_block(units, dirs[:, tile(q)], rb)
            if len(outs) == 3:
                outs[0][block(rb), tile_at(j, q)] = part
            scaled = [part[:, block(k)] * factor[block(rb), :] for k in range(TILE // LANES)]
            total = add_rows(total, jnp.concatenate(scaled, axis=1))
        put_column(column, q, total)


def columns_again(s, units, dirs, got, first, keep):
    return chunked(
        functools.partial(again_kernel, keep),
        WIDTH // CHUNK,
        [WHOLE, DIRS, WHOLE] + [ANY] * len(first),
        [WHOLE] * keep + [COLUMN],
        [shape((GROUP, WIDTH))] * keep + [shape((KB, LANES))],
        [pltpu.VMEM((GROUP, LANES), F32)],
    )(s, units, dirs, got, *first)


def col_scale(pieces):
    return 1.0 / (PROTOS * (pieces[0][...] + pieces[1][...] + pieces[2][...] + pieces[3][...]))


def row_part(mass, scale, rb):
    total = jnp.zeros((LANES, LANES), F32)
    for k in range(KB):
        total = total + mass[block(rb), block(k)] * scale[k : k + 1, :]
    return rows_to_lanes(total)


def copies(out):
    value = out[0]
    for i in range(1, out.shape[0]):
        out[i] = value


def first_row_kernel(s, units, dirs, a0, a1, a2, a3, first, out, sums):
    j = pl.program_id(0)
    n = CHUNK // LANES
    rows = pl.ds(pl.multiple_of(j * n, n), n)
    scale = 1.0 / (PROTOS * (a0[rows, :] + a1[rows, :] + a2[rows, :] + a3[rows, :]))

    @pl.when(j == 0)
    def _():
        sums[...] = jnp.zeros_like(sums)

    for q in range(CHUNK // TILE):
        for rb in range(RB):
            part = mass_block(units, dirs[:, tile(q)], rb)
            total = sums[block(rb), :]
            for k in range(TILE // LANES):
                at = q * (TILE // LANES) + k
                total = total + part[:, block(k)] * scale[at : at + 1, :]
            sums[block(rb), :] = total

    @pl.when(j == pl.num_programs(0) - 1)
    def _():
        for rb in range(RB):
            out[0, rb : rb + 1, :] = rows_to_lanes(sums[block(rb), :])
        copies(out)


def first_row_sums(s, units, dirs, pieces, first):
    return chunked(
        first_row_kernel,
        WIDTH // CHUNK,
        [WHOLE, DIRS] + [WHOLE] * 4 + [ANY],
        WHOLE,
        shape((PEERS, RB, LANES)),
        [pltpu.VMEM((GROUP, LANES), F32)],
    )(s, units, dirs, *pieces, first)


def row_kernel(mass, a0, a1, a2, a3, out):
    scale = col_scale((a0, a1, a2, a3))
    for rb in range(RB):
        out[0, rb : rb + 1, :] = row_part(mass, scale, rb)
    copies(out)


def last_row_kernel(mass, a0, a1, a2, a3, exps, out):
    scale = col_scale((a0, a1, a2, a3))
    for rb in range(RB):
        out[0, rb : rb + 1, :] = row_part(mass, scale, rb)
    out[0, RB : 2 * RB, :] = exps[...]
    copies(out)


def student_kernel(s, r0, r1, r2, r3, protos, exps, hat, dirs, sums):
    j = pl.program_id(0)
    put_dirs(protos, dirs)

    @pl.when(j == 0)
    def _():
        sums[...] = jnp.zeros_like(sums)
        for b, rows in enumerate((r0, r1, r2, r3)):
            hat[own_rows(s, b), :] = unit(rows[...], 1)[0].astype(BF16)

    for q in range(CHUNK // TILE):
        for rb in range(RB):
            part = jnp.exp(dot(hat[block(rb), :], dirs[:, tile(q)]) * (1.0 / STUDENT_TEMP))
            sums[block(rb), :] = sums[block(rb), :] + fold_lanes(part)

    @pl.when(j == pl.num_programs(0) - 1)
    def _():
        for rb in range(RB):
            exps[rb : rb + 1, :] = rows_to_lanes(sums[block(rb), :])


def student_exps(s, rows, protos):
    return chunked(
        student_kernel,
        WIDTH // CHUNK,
        [ROW_BLOCK] * NY + [proto_block(CHUNK)],
        [WHOLE, WHOLE, DIRS_OUT],
        [shape((RB, LANES)), shape((GROUP, DEPTH), BF16), far((DEPTH, WIDTH), BF16)],
        [pltpu.VMEM((GROUP, LANES), F32)],
    )(s, *rows, protos)


def pick_kernel(s, source, features, first, out):
    me = (s[0] * NY + s[1]) * NC + s[2]
    marks = lax.shift_right_logical(source[...], 8) == me
    local = jnp.bitwise_and(source[...], ROWS - 1).astype(F32)
    counts = exclusive_counts(jnp.where(marks, 1.0, 0.0))
    counts = jnp.where(marks, counts, -1.0)
    rank = lax.broadcasted_iota(jnp.int32, (PARTS, SLOT, ROWS), 1).astype(F32)
    shown = jnp.where(counts[:, None, :] == rank, local[:, None, :], 0.0)
    asked = jnp.sum(shown, axis=2, keepdims=True)
    lane = lax.broadcasted_iota(jnp.int32, (PARTS, SLOT, ROWS), 2).astype(F32)
    pick = jnp.where(asked == lane, 1.0, 0.0).reshape(ROWS, ROWS).astype(BF16)
    rows = dot(pick, features[...])
    for x in range(NX):
        for c in range(NC):
            parts = []
            for y in range(NY):
                e = ((x * NY + y) * NC + c) * SLOT
                parts.append(rows[e : e + SLOT, :])
            parcel = jnp.concatenate(parts, axis=0).astype(BF16)
            for y in range(NY):
                out[(x * NY + y) * NC + c] = parcel


def pick_rows(s, source, features, first):
    return pl.pallas_call(
        pick_kernel,
        in_specs=[pl.BlockSpec(memory_space=pltpu.SMEM), WHOLE, WHOLE, ANY],
        out_specs=WHOLE,
        out_shape=shape((PARTS, NY * SLOT, DEPTH), BF16),
        cost_estimate=COST,
        compiler_params=PARAMS,
    )(s, source, features, first)


def matched_kernel(s, source, arrived, dirs, mass, units):
    j = pl.program_id(0)

    @pl.when(j == 0)
    def _():
        index = lax.broadcasted_iota(jnp.int32, (PARTS, ROWS), 0)
        part = lax.broadcasted_iota(jnp.int32, (PARTS, ROWS), 0)
        slot = lax.broadcasted_iota(jnp.int32, (ROWS, ROWS), 0).astype(F32)
        rows = arrived[...].astype(F32)
        for y in range(NY):
            e = (s[0] * NY + y) * NC + s[2]
            mine = jnp.sum(jnp.where(index == e, source[...], 0), axis=0, keepdims=True)
            owner = lax.shift_right_logical(mine, 8)
            marks = jnp.where(part == owner, 1.0, 0.0)
            rank = jnp.sum(marks * exclusive_counts(marks), axis=0, keepdims=True)
            place = jnp.where(slot == owner.astype(F32) * SLOT + rank, 1.0, 0.0).astype(BF16)
            came = rows[:, y * SLOT : (y + 1) * SLOT, :].reshape(ROWS, DEPTH).astype(BF16)
            matched = lax.dot_general(place, came, (((0,), (0,)), ((), ())), preferred_element_type=F32)
            units[y * ROWS : (y + 1) * ROWS, :] = unit(matched, 1)[0].astype(BF16)

    for q in range(CHUNK // TILE):
        for rb in range(RB):
            mass[block(rb), tile_at(j, q)] = mass_block(units, dirs[:, tile(q)], rb)


def matched_mass(s, source, arrived, dirs):
    return chunked(
        matched_kernel,
        WIDTH // CHUNK,
        [WHOLE, WHOLE, DIRS],
        [WHOLE, WHOLE],
        [shape((GROUP, WIDTH)), shape((GROUP, DEPTH), BF16)],
    )(s, source, arrived, dirs)


def target_kernel(s, mass, a0, a1, a2, a3, got, hat, dirs, targets, exps, out, sums, cross):
    j = pl.program_id(0)
    n = CHUNK // LANES

    @pl.when(j == 0)
    def _():
        sums[...] = jnp.zeros_like(sums)
        cross[...] = jnp.zeros_like(cross)
        exps[...] = jnp.sum(got[...], axis=0)

    rows = pl.ds(pl.multiple_of(j * n, n), n)
    scale = (CROPS / PROTOS) / (a0[rows, :] + a1[rows, :] + a2[rows, :] + a3[rows, :])
    row_scale = 1.0 / (CROPS * exps[:RB, :])
    for rb in range(RB):
        factor = lanes_to_rows(row_scale[rb : rb + 1, :])
        scores = dot(hat[block(rb), :], dirs[...]) * (1.0 / STUDENT_TEMP)
        total = jnp.zeros((LANES, LANES), F32)
        crossed = jnp.zeros((LANES, LANES), F32)
        for k in range(n):
            cols = pl.ds(pl.multiple_of(j * CHUNK + k * LANES, LANES), LANES)
            value = (mass[block(rb), cols] * factor * scale[k : k + 1, :]).astype(BF16)
            targets[block(rb), cols] = value
            value = value.astype(F32)
            total = total + value
            crossed = crossed + value * scores[:, block(k)]
        sums[block(rb), :] = sums[block(rb), :] + total
        cross[...] = cross[...] + crossed

    @pl.when(j == pl.num_programs(0) - 1)
    def _():
        loss = jnp.zeros((1, LANES), F32)
        for rb in range(RB):
            total = rows_to_lanes(sums[block(rb), :])
            out[0, rb : rb + 1, :] = total
            loss = loss + total * jnp.log(exps[RB + rb : RB + rb + 1, :])
        loss = loss - jnp.sum(cross[...], axis=0, keepdims=True)
        out[0, RB : 2 * RB, :] = jnp.broadcast_to(loss, (RB, LANES))
        copies(out)


def make_targets(s, mass, pieces, got, hat, dirs):
    return chunked(
        target_kernel,
        WIDTH // CHUNK,
        [WHOLE] * 7 + [DIRS_OUT],
        [WHOLE, WHOLE, WHOLE],
        [
            shape((GROUP, WIDTH), BF16),
            shape((2 * RB, LANES)),
            shape((PEERS, 2 * RB, LANES)),
        ],
        [
            pltpu.VMEM((GROUP, LANES), F32),
            pltpu.VMEM((LANES, LANES), F32),
        ],
    )(s, mass, *pieces, got, hat, dirs)


def grad_kernel(
    s, targets, exps, got, hat, dirs, protos, r0, r1, r2, r3, f0, f1, f2, f3, keep, give, loss,
    factor, grads, turned, feature
):
    j = pl.program_id(0)

    @pl.when(j == 0)
    def _():
        totals = jnp.sum(got[...], axis=0)
        loss[...] = totals[RB:, :]
        scale = totals[:RB, :] / exps[RB:, :]
        for rb in range(RB):
            factor[block(rb), :] = lanes_to_rows(scale[rb : rb + 1, :])
        turned[...] = hat[...].astype(F32).T.astype(BF16)
        feature[...] = jnp.zeros_like(feature)

    for rb in range(RB):
        probs = jnp.exp(dot(hat[block(rb), :], dirs[...]) * (1.0 / STUDENT_TEMP))
        for k in range(GRAD_CHUNK // LANES):
            cols = pl.ds(pl.multiple_of(j * GRAD_CHUNK + k * LANES, LANES), LANES)
            came = targets[block(rb), cols].astype(F32)
            value = probs[:, block(k)] * factor[block(rb), :] - came
            grads[block(rb), block(k)] = (value * (1.0 / STUDENT_TEMP)).astype(BF16)
    feature[...] = feature[...] + lax.dot_general(
        grads[...], dirs[...], (((1,), (1,)), ((), ())), preferred_element_type=F32
    )
    weights = dot(turned[...], grads[...])
    for k in range(GRAD_CHUNK // LANES):
        weight = weights[:, block(k)]
        floats, inverse = unit(protos[:, block(k)], 0)
        stat = jnp.sum(weight * dirs[:, block(k)].astype(F32), axis=0, keepdims=True)
        weight = ((weight - floats * stat) * inverse).reshape(NX * NY, NC, DEPTH // PARTS, LANES)
        own = s[2] == 0
        keep[:, :, block(k)] = jnp.where(own, weight[:, 0], weight[:, 1])
        give[:, :, block(k)] = jnp.where(own, weight[:, 1], weight[:, 0])

    @pl.when(j == pl.num_programs(0) - 1)
    def _():
        for b, (rows, out) in enumerate(((r0, f0), (r1, f1), (r2, f2), (r3, f3))):
            units, inverse = unit(rows[...], 1)
            value = feature[own_rows(s, b), :]
            along = jnp.sum(units * value, axis=1, keepdims=True)
            out[...] = (value - units * along) * inverse


def gradients(s, targets, exps, got, hat, dirs, protos, rows):
    share = (NX * NY, DEPTH // PARTS, WIDTH)
    part = pl.BlockSpec((NX * NY, DEPTH // PARTS, GRAD_CHUNK), lambda j, s: (0, 0, j))
    return chunked(
        grad_kernel,
        WIDTH // GRAD_CHUNK,
        [WHOLE, WHOLE, WHOLE, WHOLE]
        + [pl.BlockSpec((DEPTH, GRAD_CHUNK), lambda j, s: (0, j)), proto_block(GRAD_CHUNK)]
        + [ROW_BLOCK] * NY,
        [WHOLE] * NY + [part, part, WHOLE],
        [shape((ROWS, DEPTH))] * NY + [shape(share), shape(share), shape((RB, LANES))],
        [
            pltpu.VMEM((GROUP, LANES), F32),
            pltpu.VMEM((GROUP, GRAD_CHUNK), BF16),
            pltpu.VMEM((DEPTH, GROUP), BF16),
            pltpu.VMEM((GROUP, DEPTH), F32),
        ],
    )(s, targets, exps, got, hat, dirs, protos, *rows)


def add_kernel(s, a, b, first, out):
    out[...] = a[...] + b[...]


def add_shares(s, a, b, first):
    part = pl.BlockSpec((NY, DEPTH // PARTS, WIDTH), lambda j, s: (j, 0, 0))
    return chunked(add_kernel, NX, [part, part, ANY], part, shape(a.shape))(s, a, b, first)


def join_kernel(z, *args):
    out = args[-1]
    rows = args[0].shape[0]
    for b, piece in enumerate(args[:-1]):
        k = lax.rem(z[0] // 2 - b + NZ // 2, NZ // 2) * rows
        out[pl.ds(pl.multiple_of(k, rows), rows), :] = piece[...]


def join_z(z, pieces):
    return pl.pallas_call(
        join_kernel,
        in_specs=[pl.BlockSpec(memory_space=pltpu.SMEM)] + [WHOLE] * len(pieces),
        out_specs=WHOLE,
        out_shape=shape((ROWS, DEPTH)),
        cost_estimate=COST,
        compiler_params=PARAMS,
    )(z, *pieces)


def shift(v, axis, size, step):
    return lax.ppermute(v, axis, [(i, (i + step) % size) for i in range(size)])


def gather_y(v):
    return [v] + [shift(v, "y", NY, b) for b in range(1, NY)]


def swap_rows(v):
    return lax.all_to_all(v, ("y", "z"), 0, 0, tiled=True)


def column_pieces(v):
    v = v + shift(v, "c", NC, 1)
    return [v] + [shift(v, "x", NX, b) for b in range(1, NX)]


def body(teacher_features, teacher_protos, student_features, student_protos, student_source):
    s = jnp.stack([lax.axis_index(a) for a in DP]).astype(jnp.int32)
    teacher_protos = pltpu.with_memory_space_constraint(teacher_protos, pltpu.HBM)
    student_protos = pltpu.with_memory_space_constraint(student_protos, pltpu.HBM)
    source = lax.all_to_all(
        jnp.broadcast_to(student_source[None], (PARTS, ROWS)), DP, 0, 0, tiled=True
    )
    column, dirs, units = teacher_units(s, gather_y(teacher_features), teacher_protos)
    got = swap_rows(first_row_sums(s, units, dirs, column_pieces(column), source))

    student_rows = gather_y(student_features)
    exps, hat, dirs_s = student_exps(s, student_rows, student_protos)
    dirs_s = hbm(dirs_s)
    mass, column = columns_again(s, units, dirs, got, student_rows[1:], 1)
    parts = call(row_kernel, shape((PEERS, RB, LANES)), mass, *column_pieces(column))
    got = swap_rows(parts)

    parcel = pick_rows(s, source, teacher_features, exps)
    arrived = lax.all_to_all(parcel, DP, 0, 0, tiled=True)
    (column,) = columns_again(s, units, dirs, got, [exps], 0)
    mass, _ = matched_mass(s, source, arrived, dirs)
    pieces = column_pieces(column)
    got = swap_rows(call(last_row_kernel, shape((PEERS, 2 * RB, LANES)), mass, *pieces, exps))

    targets, exps, parts = make_targets(s, mass, pieces, got, hat, dirs_s)
    got = swap_rows(parts)
    *features, keep, give, loss = gradients(
        s, targets, exps, got, hat, dirs_s, student_protos, student_rows
    )
    feature = features[0]
    for b in range(1, NY):
        feature = feature + shift(features[b], "y", NY, NY - b)
    feature = lax.all_to_all(feature.reshape(NZ, ROWS // NZ, DEPTH), "z", 0, 0, tiled=True)
    feature = jnp.sum(feature, axis=0)
    loss = functools.reduce(jnp.add, column_pieces(loss))
    weight = add_shares(s, keep, shift(give, "c", NC, 1), loss)
    weight = lax.all_to_all(weight, ("x", "y"), 0, 0, tiled=True)

    z = lax.axis_index("z").astype(jnp.int32).reshape(1)
    other = lax.ppermute(feature, "z", [(i, i ^ 1) for i in range(NZ)])
    even = z[0] % 2 == 0
    pair = jnp.concatenate([jnp.where(even, feature, other), jnp.where(even, other, feature)])
    pieces = [pair] + [shift(pair, "z", NZ, 2 * b) for b in range(1, NZ // 2)]
    grad_features = join_z(z, pieces)

    weight = jnp.sum(weight.reshape(NX, NY, DEPTH // PARTS, WIDTH), axis=0)
    grad_protos = weight.transpose(1, 0, 2).reshape(DEPTH // PARTS, NY * WIDTH)

    loss = jnp.sum(loss[0]) / CROPS
    return (loss, grad_features, grad_protos)


def solution(mesh):
    return jax.shard_map(
        body,
        mesh=Mesh(mesh.devices.reshape(NX, NY, NC, NZ), ("x", "y", "c", "z")),
        in_specs=(P(DP, None), P(None, "z"), P(DP, None), P(None, "z"), P(DP)),
        out_specs=(P(), P(DP, None), P(DP, "z")),
        check_vma=False,
    )
```

```python
import functools

import jax
import jax.numpy as jnp
from jax import lax
from jax.experimental import pallas as pl
from jax.experimental.pallas import tpu as pltpu
from jax.sharding import Mesh, PartitionSpec as P

PROTOS = 65536
CROPS = 8192
ITERS = 3
NX, NY, NC, NZ = 4, 4, 2, 8
DP = ("x", "y", "c")
PARTS = NX * NY * NC
ROWS = CROPS // PARTS
SLOT = ROWS // PARTS
DEPTH = 256
GROUP = NY * ROWS
WIDTH = PROTOS // (NY * NZ)
SPAN = PROTOS // NZ
CHUNK = 1024
GRAD_CHUNK = 512
LANES = 128
TILE = 256
RB = GROUP // LANES
KB = WIDTH // LANES
OWN = ROWS // LANES
PEERS = NY * NZ

TEACHER_TEMP = 0.04
STUDENT_TEMP = 0.1
NORM_EPSILON = 1e-06
F32 = jnp.float32
BF16 = jnp.bfloat16

WHOLE = pl.BlockSpec(memory_space=pltpu.VMEM)
PARAMS = pltpu.CompilerParams(vmem_limit_bytes=30 << 20)
COST = pl.CostEstimate(flops=0, bytes_accessed=36000, transcendentals=0)
ROW_BLOCK = pl.BlockSpec((ROWS, DEPTH), lambda j, s: (0, 0))


def proto_block(chunk):
    return split_rows(DEPTH, chunk, 4, lambda j, s: s[1] * (WIDTH // chunk) + j)


def call(kernel, out_shape, *args):
    return pl.pallas_call(
        kernel,
        in_specs=[WHOLE] * len(args),
        out_specs=jax.tree.map(lambda _: WHOLE, out_shape),
        out_shape=out_shape,
        cost_estimate=COST,
        compiler_params=PARAMS,
    )(*args)


class Joined:
    def __init__(self, refs):
        self.refs = refs

    @property
    def shape(self):
        return (sum(r.shape[0] for r in self.refs), self.refs[0].shape[1])

    def __getitem__(self, at):
        return jnp.concatenate([r[at] for r in self.refs], axis=0)


def split_rows(rows, columns, parts, place):
    def spec(r):
        return pl.BlockSpec((rows // parts, columns), lambda j, s: (r, place(j, s)))

    return [spec(r) for r in range(parts)]


def chunked(kernel, steps, in_specs, out_specs, out_shape, scratch=()):
    groups = [spec if isinstance(spec, list) else [spec] for spec in in_specs]

    def regrouped(s, *refs):
        refs, args = list(refs), []
        for spec, group in zip(in_specs, groups):
            mine, refs = refs[: len(group)], refs[len(group) :]
            args.append(Joined(mine) if isinstance(spec, list) else mine[0])
        return kernel(s, *args, *refs)

    run = pl.pallas_call(
        regrouped,
        grid_spec=pltpu.PrefetchScalarGridSpec(
            num_scalar_prefetch=1,
            grid=(steps,),
            in_specs=[spec for group in groups for spec in group],
            out_specs=out_specs,
            scratch_shapes=scratch,
        ),
        out_shape=out_shape,
        cost_estimate=COST,
        compiler_params=PARAMS,
    )

    def apply(s, *args):
        return run(s, *[a for a, group in zip(args, groups, strict=True) for _ in group])

    return apply


def shape(dims, dtype=F32):
    return jax.ShapeDtypeStruct(dims, dtype)


def far(dims, dtype=F32):
    return pltpu.HBM(dims, dtype)


def hbm(v):
    return pltpu.with_memory_space_constraint(v, pltpu.HBM)


def unit(values, axis):
    floats = values.astype(F32)
    inverse = 1.0 / jnp.sqrt(jnp.sum(floats * floats, axis=axis, keepdims=True) + NORM_EPSILON)
    return floats * inverse, inverse


def own_rows(s, b):
    return pl.ds(pl.multiple_of(lax.rem(s[1] - b + NY, NY) * ROWS, ROWS), ROWS)


def block(rb):
    return slice(rb * LANES, (rb + 1) * LANES)


def tile(q):
    return slice(q * TILE, (q + 1) * TILE)


def tile_at(j, q):
    return pl.ds(pl.multiple_of(j * CHUNK + q * TILE, TILE), TILE)


def put_dirs(protos, dirs):
    width = protos.shape[1]
    sums = []
    for k in range(width // LANES):
        floats = protos[:, block(k)].astype(F32)
        parts = (floats * floats).reshape(4, DEPTH // 32, 8, LANES)
        sums.append(jnp.sum(jnp.sum(parts, axis=1), axis=0))
    total = jnp.sum(jnp.concatenate(sums, axis=1), axis=0, keepdims=True)
    inverse = 1.0 / jnp.sqrt(total + NORM_EPSILON)
    for k in range(width // LANES):
        dirs[:, block(k)] = (protos[:, block(k)].astype(F32) * inverse[:, block(k)]).astype(BF16)


def lanes_to_rows(row):
    return jnp.broadcast_to(row, (LANES, LANES)).T


def fold_lanes(values):
    return functools.reduce(jnp.add, [values[:, block(k)] for k in range(values.shape[1] // LANES)])


def rows_to_lanes(values):
    return jnp.sum(values.T, axis=0, keepdims=True)


def dot(a, b):
    return jnp.dot(a, b, preferred_element_type=F32)


def exclusive_counts(marks):
    n = marks.shape[1]
    before = lax.broadcasted_iota(jnp.int32, (n, n), 0) < lax.broadcasted_iota(jnp.int32, (n, n), 1)
    return dot(marks.astype(BF16), before.astype(BF16))


def mass_block(units, dirs, rb):
    return jnp.exp(dot(units[block(rb), :], dirs) * (1.0 / TEACHER_TEMP))


def put_column(column, q, total):
    total = jnp.sum(total, axis=0, keepdims=True)
    for k in range(TILE // LANES):
        row = q * (TILE // LANES) + k
        column[row : row + 1, :] = total[:, block(k)]


def add_rows(total, part):
    return total + jnp.sum(part.reshape(LANES // 8, 8, TILE), axis=0)


def mass_kernel(s, r0, r1, r2, r3, protos, column, dirs, units):
    j = pl.program_id(0)

    @pl.when(j == 0)
    def _():
        for b, rows in enumerate((r0, r1, r2, r3)):
            units[own_rows(s, b), :] = unit(rows[...], 1)[0].astype(BF16)

    put_dirs(protos, dirs)
    for q in range(CHUNK // TILE):
        total = jnp.zeros((8, TILE), F32)
        for rb in range(RB):
            total = add_rows(total, mass_block(units, dirs[:, tile(q)], rb))
        put_column(column, q, total)


COLUMN = pl.BlockSpec((CHUNK // LANES, LANES), lambda j, s: (j, 0))
DIRS_OUT = pl.BlockSpec((DEPTH, CHUNK), lambda j, s: (0, j))
DIRS = split_rows(DEPTH, CHUNK, 4, lambda j, s: j)
ANY = pl.BlockSpec(memory_space=pl.ANY)
GROUP_ROWS = pl.BlockSpec((GROUP, CHUNK), lambda j, s: (0, j))


def teacher_units(s, rows, protos):
    return chunked(
        mass_kernel,
        WIDTH // CHUNK,
        [ROW_BLOCK] * NY + [proto_block(CHUNK)],
        [COLUMN, DIRS_OUT, WHOLE],
        [
            shape((KB, LANES)),
            shape((DEPTH, WIDTH), BF16),
            shape((GROUP, DEPTH), BF16),
        ],
    )(s, *rows, protos)


def again_kernel(keep, s, units, dirs, got, *rest):
    j = pl.program_id(0)
    outs = rest[-3 if keep else -2 :]
    column, factor = outs[-2:]

    @pl.when(j == 0)
    def _():
        scale = 1.0 / (CROPS * jnp.sum(got[...], axis=0))
        for rb in range(RB):
            factor[block(rb), :] = lanes_to_rows(scale[rb : rb + 1, :])

    for q in range(CHUNK // TILE):
        total = jnp.zeros((8, TILE), F32)
        for rb in range(RB):
            part = mass_block(units, dirs[:, tile(q)], rb)
            if len(outs) == 3:
                outs[0][block(rb), tile_at(j, q)] = part
            scaled = [part[:, block(k)] * factor[block(rb), :] for k in range(TILE // LANES)]
            total = add_rows(total, jnp.concatenate(scaled, axis=1))
        put_column(column, q, total)


def columns_again(s, units, dirs, got, first, keep):
    return chunked(
        functools.partial(again_kernel, keep),
        WIDTH // CHUNK,
        [WHOLE, DIRS, WHOLE] + [ANY] * len(first),
        [WHOLE] * keep + [COLUMN],
        [shape((GROUP, WIDTH))] * keep + [shape((KB, LANES))],
        [pltpu.VMEM((GROUP, LANES), F32)],
    )(s, units, dirs, got, *first)


def col_scale(pieces):
    return 1.0 / (PROTOS * (pieces[0][...] + pieces[1][...] + pieces[2][...] + pieces[3][...]))


def row_part(mass, scale, rb):
    total = jnp.zeros((LANES, LANES), F32)
    for k in range(KB):
        total = total + mass[block(rb), block(k)] * scale[k : k + 1, :]
    return rows_to_lanes(total)


def copies(out):
    value = out[0]
    for i in range(1, out.shape[0]):
        out[i] = value


def first_row_kernel(s, units, dirs, a0, a1, a2, a3, first, out, sums):
    j = pl.program_id(0)
    n = CHUNK // LANES
    rows = pl.ds(pl.multiple_of(j * n, n), n)
    scale = 1.0 / (PROTOS * (a0[rows, :] + a1[rows, :] + a2[rows, :] + a3[rows, :]))

    @pl.when(j == 0)
    def _():
        sums[...] = jnp.zeros_like(sums)

    for q in range(CHUNK // TILE):
        for rb in range(RB):
            part = mass_block(units, dirs[:, tile(q)], rb)
            total = sums[block(rb), :]
            for k in range(TILE // LANES):
                at = q * (TILE // LANES) + k
                total = total + part[:, block(k)] * scale[at : at + 1, :]
            sums[block(rb), :] = total

    @pl.when(j == pl.num_programs(0) - 1)
    def _():
        for rb in range(RB):
            out[0, rb : rb + 1, :] = rows_to_lanes(sums[block(rb), :])
        copies(out)


def first_row_sums(s, units, dirs, pieces, first):
    return chunked(
        first_row_kernel,
        WIDTH // CHUNK,
        [WHOLE, DIRS] + [WHOLE] * 4 + [ANY],
        WHOLE,
        shape((PEERS, RB, LANES)),
        [pltpu.VMEM((GROUP, LANES), F32)],
    )(s, units, dirs, *pieces, first)


def row_kernel(mass, a0, a1, a2, a3, out):
    scale = col_scale((a0, a1, a2, a3))
    for rb in range(RB):
        out[0, rb : rb + 1, :] = row_part(mass, scale, rb)
    copies(out)


def last_row_kernel(mass, a0, a1, a2, a3, exps, out):
    scale = col_scale((a0, a1, a2, a3))
    for rb in range(RB):
        out[0, rb : rb + 1, :] = row_part(mass, scale, rb)
    out[0, RB : 2 * RB, :] = exps[...]
    copies(out)


def student_kernel(s, r0, r1, r2, r3, protos, exps, hat, dirs, sums):
    j = pl.program_id(0)
    put_dirs(protos, dirs)

    @pl.when(j == 0)
    def _():
        sums[...] = jnp.zeros_like(sums)
        for b, rows in enumerate((r0, r1, r2, r3)):
            hat[own_rows(s, b), :] = unit(rows[...], 1)[0].astype(BF16)

    for q in range(CHUNK // TILE):
        for rb in range(RB):
            part = jnp.exp(dot(hat[block(rb), :], dirs[:, tile(q)]) * (1.0 / STUDENT_TEMP))
            sums[block(rb), :] = sums[block(rb), :] + fold_lanes(part)

    @pl.when(j == pl.num_programs(0) - 1)
    def _():
        for rb in range(RB):
            exps[rb : rb + 1, :] = rows_to_lanes(sums[block(rb), :])


def student_exps(s, rows, protos):
    return chunked(
        student_kernel,
        WIDTH // CHUNK,
        [ROW_BLOCK] * NY + [proto_block(CHUNK)],
        [WHOLE, WHOLE, DIRS_OUT],
        [shape((RB, LANES)), shape((GROUP, DEPTH), BF16), far((DEPTH, WIDTH), BF16)],
        [pltpu.VMEM((GROUP, LANES), F32)],
    )(s, *rows, protos)


def pick_kernel(s, source, features, first, out):
    me = (s[0] * NY + s[1]) * NC + s[2]
    marks = lax.shift_right_logical(source[...], 8) == me
    local = jnp.bitwise_and(source[...], ROWS - 1).astype(F32)
    counts = exclusive_counts(jnp.where(marks, 1.0, 0.0))
    counts = jnp.where(marks, counts, -1.0)
    rank = lax.broadcasted_iota(jnp.int32, (PARTS, SLOT, ROWS), 1).astype(F32)
    shown = jnp.where(counts[:, None, :] == rank, local[:, None, :], 0.0)
    asked = jnp.sum(shown, axis=2, keepdims=True)
    lane = lax.broadcasted_iota(jnp.int32, (PARTS, SLOT, ROWS), 2).astype(F32)
    pick = jnp.where(asked == lane, 1.0, 0.0).reshape(ROWS, ROWS).astype(BF16)
    rows = dot(pick, features[...])
    for x in range(NX):
        for c in range(NC):
            parts = []
            for y in range(NY):
                e = ((x * NY + y) * NC + c) * SLOT
                parts.append(rows[e : e + SLOT, :])
            parcel = jnp.concatenate(parts, axis=0).astype(BF16)
            for y in range(NY):
                out[(x * NY + y) * NC + c] = parcel


def pick_rows(s, source, features, first):
    return pl.pallas_call(
        pick_kernel,
        in_specs=[pl.BlockSpec(memory_space=pltpu.SMEM), WHOLE, WHOLE, ANY],
        out_specs=WHOLE,
        out_shape=shape((PARTS, NY * SLOT, DEPTH), BF16),
        cost_estimate=COST,
        compiler_params=PARAMS,
    )(s, source, features, first)


def matched_kernel(s, source, arrived, dirs, mass, units):
    j = pl.program_id(0)

    @pl.when(j == 0)
    def _():
        index = lax.broadcasted_iota(jnp.int32, (PARTS, ROWS), 0)
        part = lax.broadcasted_iota(jnp.int32, (PARTS, ROWS), 0)
        slot = lax.broadcasted_iota(jnp.int32, (ROWS, ROWS), 0).astype(F32)
        rows = arrived[...].astype(F32)
        for y in range(NY):
            e = (s[0] * NY + y) * NC + s[2]
            mine = jnp.sum(jnp.where(index == e, source[...], 0), axis=0, keepdims=True)
            owner = lax.shift_right_logical(mine, 8)
            marks = jnp.where(part == owner, 1.0, 0.0)
            rank = jnp.sum(marks * exclusive_counts(marks), axis=0, keepdims=True)
            place = jnp.where(slot == owner.astype(F32) * SLOT + rank, 1.0, 0.0).astype(BF16)
            came = rows[:, y * SLOT : (y + 1) * SLOT, :].reshape(ROWS, DEPTH).astype(BF16)
            matched = lax.dot_general(place, came, (((0,), (0,)), ((), ())), preferred_element_type=F32)
            units[y * ROWS : (y + 1) * ROWS, :] = unit(matched, 1)[0].astype(BF16)

    for q in range(CHUNK // TILE):
        for rb in range(RB):
            mass[block(rb), tile_at(j, q)] = mass_block(units, dirs[:, tile(q)], rb)


def matched_mass(s, source, arrived, dirs):
    return chunked(
        matched_kernel,
        WIDTH // CHUNK,
        [WHOLE, WHOLE, DIRS],
        [WHOLE, WHOLE],
        [shape((GROUP, WIDTH)), shape((GROUP, DEPTH), BF16)],
    )(s, source, arrived, dirs)


def target_kernel(s, mass, a0, a1, a2, a3, got, hat, dirs, targets, exps, out, sums, cross):
    j = pl.program_id(0)
    n = CHUNK // LANES

    @pl.when(j == 0)
    def _():
        sums[...] = jnp.zeros_like(sums)
        cross[...] = jnp.zeros_like(cross)
        exps[...] = jnp.sum(got[...], axis=0)

    rows = pl.ds(pl.multiple_of(j * n, n), n)
    scale = (CROPS / PROTOS) / (a0[rows, :] + a1[rows, :] + a2[rows, :] + a3[rows, :])
    row_scale = 1.0 / (CROPS * exps[:RB, :])
    for rb in range(RB):
        factor = lanes_to_rows(row_scale[rb : rb + 1, :])
        scores = dot(hat[block(rb), :], dirs[...]) * (1.0 / STUDENT_TEMP)
        total = jnp.zeros((LANES, LANES), F32)
        crossed = jnp.zeros((LANES, LANES), F32)
        for k in range(n):
            cols = pl.ds(pl.multiple_of(j * CHUNK + k * LANES, LANES), LANES)
            value = (mass[block(rb), cols] * factor * scale[k : k + 1, :]).astype(BF16)
            targets[block(rb), cols] = value
            value = value.astype(F32)
            total = total + value
            crossed = crossed + value * scores[:, block(k)]
        sums[block(rb), :] = sums[block(rb), :] + total
        cross[...] = cross[...] + crossed

    @pl.when(j == pl.num_programs(0) - 1)
    def _():
        loss = jnp.zeros((1, LANES), F32)
        for rb in range(RB):
            total = rows_to_lanes(sums[block(rb), :])
            out[0, rb : rb + 1, :] = total
            loss = loss + total * jnp.log(exps[RB + rb : RB + rb + 1, :])
        loss = loss - jnp.sum(cross[...], axis=0, keepdims=True)
        out[0, RB : 2 * RB, :] = jnp.broadcast_to(loss, (RB, LANES))
        copies(out)


def make_targets(s, mass, pieces, got, hat, dirs):
    return chunked(
        target_kernel,
        WIDTH // CHUNK,
        [WHOLE] * 7 + [DIRS_OUT],
        [WHOLE, WHOLE, WHOLE],
        [
            shape((GROUP, WIDTH), BF16),
            shape((2 * RB, LANES)),
            shape((PEERS, 2 * RB, LANES)),
        ],
        [
            pltpu.VMEM((GROUP, LANES), F32),
            pltpu.VMEM((LANES, LANES), F32),
        ],
    )(s, mass, *pieces, got, hat, dirs)


def grad_kernel(
    s, targets, exps, got, hat, dirs, protos, r0, r1, r2, r3, f0, f1, f2, f3, keep, give, loss,
    factor, grads, turned, feature
):
    j = pl.program_id(0)

    @pl.when(j == 0)
    def _():
        totals = jnp.sum(got[...], axis=0)
        loss[...] = totals[RB:, :]
        scale = totals[:RB, :] / exps[RB:, :]
        for rb in range(RB):
            factor[block(rb), :] = lanes_to_rows(scale[rb : rb + 1, :])
        turned[...] = hat[...].astype(F32).T.astype(BF16)
        feature[...] = jnp.zeros_like(feature)

    for rb in range(RB):
        probs = jnp.exp(dot(hat[block(rb), :], dirs[...]) * (1.0 / STUDENT_TEMP))
        for k in range(GRAD_CHUNK // LANES):
            cols = pl.ds(pl.multiple_of(j * GRAD_CHUNK + k * LANES, LANES), LANES)
            came = targets[block(rb), cols].astype(F32)
            value = probs[:, block(k)] * factor[block(rb), :] - came
            grads[block(rb), block(k)] = (value * (1.0 / STUDENT_TEMP)).astype(BF16)
    feature[...] = feature[...] + lax.dot_general(
        grads[...], dirs[...], (((1,), (1,)), ((), ())), preferred_element_type=F32
    )
    weights = dot(turned[...], grads[...])
    for k in range(GRAD_CHUNK // LANES):
        weight = weights[:, block(k)]
        floats, inverse = unit(protos[:, block(k)], 0)
        stat = jnp.sum(weight * dirs[:, block(k)].astype(F32), axis=0, keepdims=True)
        weight = ((weight - floats * stat) * inverse).reshape(NX * NY, NC, DEPTH // PARTS, LANES)
        own = s[2] == 0
        keep[:, :, block(k)] = jnp.where(own, weight[:, 0], weight[:, 1])
        give[:, :, block(k)] = jnp.where(own, weight[:, 1], weight[:, 0])

    @pl.when(j == pl.num_programs(0) - 1)
    def _():
        for b, (rows, out) in enumerate(((r0, f0), (r1, f1), (r2, f2), (r3, f3))):
            units, inverse = unit(rows[...], 1)
            value = feature[own_rows(s, b), :]
            along = jnp.sum(units * value, axis=1, keepdims=True)
            out[...] = (value - units * along) * inverse


def gradients(s, targets, exps, got, hat, dirs, protos, rows):
    share = (NX * NY, DEPTH // PARTS, WIDTH)
    part = pl.BlockSpec((NX * NY, DEPTH // PARTS, GRAD_CHUNK), lambda j, s: (0, 0, j))
    return chunked(
        grad_kernel,
        WIDTH // GRAD_CHUNK,
        [WHOLE, WHOLE, WHOLE, WHOLE]
        + [pl.BlockSpec((DEPTH, GRAD_CHUNK), lambda j, s: (0, j)), proto_block(GRAD_CHUNK)]
        + [ROW_BLOCK] * NY,
        [WHOLE] * NY + [part, part, WHOLE],
        [shape((ROWS, DEPTH))] * NY + [shape(share), shape(share), shape((RB, LANES))],
        [
            pltpu.VMEM((GROUP, LANES), F32),
            pltpu.VMEM((GROUP, GRAD_CHUNK), BF16),
            pltpu.VMEM((DEPTH, GROUP), BF16),
            pltpu.VMEM((GROUP, DEPTH), F32),
        ],
    )(s, targets, exps, got, hat, dirs, protos, *rows)


def add_kernel(s, a, b, first, out):
    out[...] = a[...] + b[...]


def add_shares(s, a, b, first):
    part = pl.BlockSpec((NY, DEPTH // PARTS, WIDTH), lambda j, s: (j, 0, 0))
    return chunked(add_kernel, NX, [part, part, ANY], part, shape(a.shape))(s, a, b, first)


def join_kernel(z, *args):
    out = args[-1]
    rows = args[0].shape[0]
    for b, piece in enumerate(args[:-1]):
        k = lax.rem(z[0] // 2 - b + NZ // 2, NZ // 2) * rows
        out[pl.ds(pl.multiple_of(k, rows), rows), :] = piece[...]


def join_z(z, pieces):
    return pl.pallas_call(
        join_kernel,
        in_specs=[pl.BlockSpec(memory_space=pltpu.SMEM)] + [WHOLE] * len(pieces),
        out_specs=WHOLE,
        out_shape=shape((ROWS, DEPTH)),
        cost_estimate=COST,
        compiler_params=PARAMS,
    )(z, *pieces)


def shift(v, axis, size, step):
    return lax.ppermute(v, axis, [(i, (i + step) % size) for i in range(size)])


def gather_y(v):
    return [v] + [shift(v, "y", NY, b) for b in range(1, NY)]


def swap_rows(v):
    return lax.all_to_all(v, ("y", "z"), 0, 0, tiled=True)


def column_pieces(v):
    v = v + shift(v, "c", NC, 1)
    return [v] + [shift(v, "x", NX, b) for b in range(1, NX)]


def body(teacher_features, teacher_protos, student_features, student_protos, student_source):
    s = jnp.stack([lax.axis_index(a) for a in DP]).astype(jnp.int32)
    teacher_protos = pltpu.with_memory_space_constraint(teacher_protos, pltpu.HBM)
    student_protos = pltpu.with_memory_space_constraint(student_protos, pltpu.HBM)
    source = lax.all_to_all(
        jnp.broadcast_to(student_source[None], (PARTS, ROWS)), DP, 0, 0, tiled=True
    )
    column, dirs, units = teacher_units(s, gather_y(teacher_features), teacher_protos)
    got = swap_rows(first_row_sums(s, units, dirs, column_pieces(column), source))

    student_rows = gather_y(student_features)
    exps, hat, dirs_s = student_exps(s, student_rows, student_protos)
    dirs_s = hbm(dirs_s)
    mass, column = columns_again(s, units, dirs, got, [source], 1)
    parts = call(row_kernel, shape((PEERS, RB, LANES)), mass, *column_pieces(column))
    got = swap_rows(parts)

    parcel = pick_rows(s, source, teacher_features, exps)
    arrived = lax.all_to_all(parcel, DP, 0, 0, tiled=True)
    (column,) = columns_again(s, units, dirs, got, [exps], 0)
    mass, _ = matched_mass(s, source, arrived, dirs)
    pieces = column_pieces(column)
    got = swap_rows(call(last_row_kernel, shape((PEERS, 2 * RB, LANES)), mass, *pieces, exps))

    targets, exps, parts = make_targets(s, mass, pieces, got, hat, dirs_s)
    got = swap_rows(parts)
    *features, keep, give, loss = gradients(
        s, targets, exps, got, hat, dirs_s, student_protos, student_rows
    )
    feature = features[0]
    for b in range(1, NY):
        feature = feature + shift(features[b], "y", NY, NY - b)
    feature = lax.all_to_all(feature.reshape(NZ, ROWS // NZ, DEPTH), "z", 0, 0, tiled=True)
    feature = jnp.sum(feature, axis=0)
    loss = functools.reduce(jnp.add, column_pieces(loss))
    weight = add_shares(s, keep, shift(give, "c", NC, 1), loss)
    weight = lax.all_to_all(weight, ("x", "y"), 0, 0, tiled=True)

    z = lax.axis_index("z").astype(jnp.int32).reshape(1)
    other = lax.ppermute(feature, "z", [(i, i ^ 1) for i in range(NZ)])
    even = z[0] % 2 == 0
    pair = jnp.concatenate([jnp.where(even, feature, other), jnp.where(even, other, feature)])
    pieces = [pair] + [shift(pair, "z", NZ, 2 * b) for b in range(1, NZ // 2)]
    grad_features = join_z(z, pieces)

    weight = jnp.sum(weight.reshape(NX, NY, DEPTH // PARTS, WIDTH), axis=0)
    grad_protos = weight.transpose(1, 0, 2).reshape(DEPTH // PARTS, NY * WIDTH)

    loss = jnp.sum(loss[0]) / CROPS
    return (loss, grad_features, grad_protos)


def solution(mesh):
    return jax.shard_map(
        body,
        mesh=Mesh(mesh.devices.reshape(NX, NY, NC, NZ), ("x", "y", "c", "z")),
        in_specs=(P(DP, None), P(None, "z"), P(DP, None), P(None, "z"), P(DP)),
        out_specs=(P(), P(DP, None), P(DP, "z")),
        check_vma=False,
    )
```

```python
import functools

import jax
import jax.numpy as jnp
from jax import lax
from jax.experimental import pallas as pl
from jax.experimental.pallas import tpu as pltpu
from jax.sharding import Mesh, PartitionSpec as P

PROTOS = 65536
CROPS = 8192
ITERS = 3
NX, NY, NC, NZ = 4, 4, 2, 8
DP = ("x", "y", "c")
PARTS = NX * NY * NC
ROWS = CROPS // PARTS
SLOT = ROWS // PARTS
DEPTH = 256
GROUP = NY * ROWS
WIDTH = PROTOS // (NY * NZ)
SPAN = PROTOS // NZ
CHUNK = 1024
GRAD_CHUNK = 512
LANES = 128
TILE = 256
RB = GROUP // LANES
KB = WIDTH // LANES
OWN = ROWS // LANES
PEERS = NY * NZ

TEACHER_TEMP = 0.04
STUDENT_TEMP = 0.1
NORM_EPSILON = 1e-06
F32 = jnp.float32
BF16 = jnp.bfloat16

WHOLE = pl.BlockSpec(memory_space=pltpu.VMEM)
PARAMS = pltpu.CompilerParams(vmem_limit_bytes=30 << 20)
COST = pl.CostEstimate(flops=0, bytes_accessed=36000, transcendentals=0)
ROW_BLOCK = pl.BlockSpec((ROWS, DEPTH), lambda j, s: (0, 0))
STUDENT_BLOCK = pl.BlockSpec((ROWS, DEPTH), lambda j, s: (0, 1))


def proto_block(chunk):
    return split_rows(DEPTH, chunk, 4, lambda j, s: s[1] * (WIDTH // chunk) + j)


def call(kernel, out_shape, *args):
    return pl.pallas_call(
        kernel,
        in_specs=[WHOLE] * len(args),
        out_specs=jax.tree.map(lambda _: WHOLE, out_shape),
        out_shape=out_shape,
        cost_estimate=COST,
        compiler_params=PARAMS,
    )(*args)


class Joined:
    def __init__(self, refs):
        self.refs = refs

    @property
    def shape(self):
        return (sum(r.shape[0] for r in self.refs), self.refs[0].shape[1])

    def __getitem__(self, at):
        return jnp.concatenate([r[at] for r in self.refs], axis=0)


def split_rows(rows, columns, parts, place):
    def spec(r):
        return pl.BlockSpec((rows // parts, columns), lambda j, s: (r, place(j, s)))

    return [spec(r) for r in range(parts)]


def chunked(kernel, steps, in_specs, out_specs, out_shape, scratch=()):
    groups = [spec if isinstance(spec, list) else [spec] for spec in in_specs]

    def regrouped(s, *refs):
        refs, args = list(refs), []
        for spec, group in zip(in_specs, groups):
            mine, refs = refs[: len(group)], refs[len(group) :]
            args.append(Joined(mine) if isinstance(spec, list) else mine[0])
        return kernel(s, *args, *refs)

    run = pl.pallas_call(
        regrouped,
        grid_spec=pltpu.PrefetchScalarGridSpec(
            num_scalar_prefetch=1,
            grid=(steps,),
            in_specs=[spec for group in groups for spec in group],
            out_specs=out_specs,
            scratch_shapes=scratch,
        ),
        out_shape=out_shape,
        cost_estimate=COST,
        compiler_params=PARAMS,
    )

    def apply(s, *args):
        return run(s, *[a for a, group in zip(args, groups, strict=True) for _ in group])

    return apply


def shape(dims, dtype=F32):
    return jax.ShapeDtypeStruct(dims, dtype)


def far(dims, dtype=F32):
    return pltpu.HBM(dims, dtype)


def hbm(v):
    return pltpu.with_memory_space_constraint(v, pltpu.HBM)


def unit(values, axis):
    floats = values.astype(F32)
    inverse = 1.0 / jnp.sqrt(jnp.sum(floats * floats, axis=axis, keepdims=True) + NORM_EPSILON)
    return floats * inverse, inverse


def own_rows(s, b):
    return pl.ds(pl.multiple_of(lax.rem(s[1] - b + NY, NY) * ROWS, ROWS), ROWS)


def block(rb):
    return slice(rb * LANES, (rb + 1) * LANES)


def tile(q):
    return slice(q * TILE, (q + 1) * TILE)


def tile_at(j, q):
    return pl.ds(pl.multiple_of(j * CHUNK + q * TILE, TILE), TILE)


def put_dirs(protos, dirs):
    width = protos.shape[1]
    sums = []
    for k in range(width // LANES):
        floats = protos[:, block(k)].astype(F32)
        parts = (floats * floats).reshape(4, DEPTH // 32, 8, LANES)
        sums.append(jnp.sum(jnp.sum(parts, axis=1), axis=0))
    total = jnp.sum(jnp.concatenate(sums, axis=1), axis=0, keepdims=True)
    inverse = 1.0 / jnp.sqrt(total + NORM_EPSILON)
    for k in range(width // LANES):
        dirs[:, block(k)] = (protos[:, block(k)].astype(F32) * inverse[:, block(k)]).astype(BF16)


def lanes_to_rows(row):
    return jnp.broadcast_to(row, (LANES, LANES)).T


def fold_lanes(values):
    return functools.reduce(jnp.add, [values[:, block(k)] for k in range(values.shape[1] // LANES)])


def rows_to_lanes(values):
    return jnp.sum(values.T, axis=0, keepdims=True)


def dot(a, b):
    return jnp.dot(a, b, preferred_element_type=F32)


def exclusive_counts(marks):
    n = marks.shape[1]
    before = lax.broadcasted_iota(jnp.int32, (n, n), 0) < lax.broadcasted_iota(jnp.int32, (n, n), 1)
    return dot(marks.astype(BF16), before.astype(BF16))


def mass_block(units, dirs, rb):
    return jnp.exp(dot(units[block(rb), :], dirs) * (1.0 / TEACHER_TEMP))


def put_column(column, q, total):
    total = jnp.sum(total, axis=0, keepdims=True)
    for k in range(TILE // LANES):
        row = q * (TILE // LANES) + k
        column[row : row + 1, :] = total[:, block(k)]


def add_rows(total, part):
    return total + jnp.sum(part.reshape(LANES // 8, 8, TILE), axis=0)


def mass_kernel(s, r0, r1, r2, r3, protos, column, dirs, units):
    j = pl.program_id(0)

    @pl.when(j == 0)
    def _():
        for b, rows in enumerate((r0, r1, r2, r3)):
            units[own_rows(s, b), :] = unit(rows[...], 1)[0].astype(BF16)

    put_dirs(protos, dirs)
    for q in range(CHUNK // TILE):
        total = jnp.zeros((8, TILE), F32)
        for rb in range(RB):
            total = add_rows(total, mass_block(units, dirs[:, tile(q)], rb))
        put_column(column, q, total)


COLUMN = pl.BlockSpec((CHUNK // LANES, LANES), lambda j, s: (j, 0))
DIRS_OUT = pl.BlockSpec((DEPTH, CHUNK), lambda j, s: (0, j))
DIRS = split_rows(DEPTH, CHUNK, 4, lambda j, s: j)
ANY = pl.BlockSpec(memory_space=pl.ANY)
GROUP_ROWS = pl.BlockSpec((GROUP, CHUNK), lambda j, s: (0, j))


def teacher_units(s, rows, protos):
    return chunked(
        mass_kernel,
        WIDTH // CHUNK,
        [ROW_BLOCK] * NY + [proto_block(CHUNK)],
        [COLUMN, DIRS_OUT, WHOLE],
        [
            shape((KB, LANES)),
            shape((DEPTH, WIDTH), BF16),
            shape((GROUP, DEPTH), BF16),
        ],
    )(s, *rows, protos)


def again_kernel(keep, s, units, dirs, got, *rest):
    j = pl.program_id(0)
    outs = rest[-3 if keep else -2 :]
    column, factor = outs[-2:]

    @pl.when(j == 0)
    def _():
        scale = 1.0 / (CROPS * jnp.sum(got[...], axis=0))
        for rb in range(RB):
            factor[block(rb), :] = lanes_to_rows(scale[rb : rb + 1, :])

    for q in range(CHUNK // TILE):
        total = jnp.zeros((8, TILE), F32)
        for rb in range(RB):
            part = mass_block(units, dirs[:, tile(q)], rb)
            if len(outs) == 3:
                outs[0][block(rb), tile_at(j, q)] = part
            scaled = [part[:, block(k)] * factor[block(rb), :] for k in range(TILE // LANES)]
            total = add_rows(total, jnp.concatenate(scaled, axis=1))
        put_column(column, q, total)


def columns_again(s, units, dirs, got, first, keep):
    return chunked(
        functools.partial(again_kernel, keep),
        WIDTH // CHUNK,
        [WHOLE, DIRS, WHOLE] + [ANY] * len(first),
        [WHOLE] * keep + [COLUMN],
        [shape((GROUP, WIDTH))] * keep + [shape((KB, LANES))],
        [pltpu.VMEM((GROUP, LANES), F32)],
    )(s, units, dirs, got, *first)


def col_scale(pieces):
    return 1.0 / (PROTOS * (pieces[0][...] + pieces[1][...] + pieces[2][...] + pieces[3][...]))


def row_part(mass, scale, rb):
    total = jnp.zeros((LANES, LANES), F32)
    for k in range(KB):
        total = total + mass[block(rb), block(k)] * scale[k : k + 1, :]
    return rows_to_lanes(total)


def copies(out):
    value = out[0]
    for i in range(1, out.shape[0]):
        out[i] = value


def first_row_kernel(s, units, dirs, a0, a1, a2, a3, first, out, sums):
    j = pl.program_id(0)
    n = CHUNK // LANES
    rows = pl.ds(pl.multiple_of(j * n, n), n)
    scale = 1.0 / (PROTOS * (a0[rows, :] + a1[rows, :] + a2[rows, :] + a3[rows, :]))

    @pl.when(j == 0)
    def _():
        sums[...] = jnp.zeros_like(sums)

    for q in range(CHUNK // TILE):
        for rb in range(RB):
            part = mass_block(units, dirs[:, tile(q)], rb)
            total = sums[block(rb), :]
            for k in range(TILE // LANES):
                at = q * (TILE // LANES) + k
                total = total + part[:, block(k)] * scale[at : at + 1, :]
            sums[block(rb), :] = total

    @pl.when(j == pl.num_programs(0) - 1)
    def _():
        for rb in range(RB):
            out[0, rb : rb + 1, :] = rows_to_lanes(sums[block(rb), :])
        copies(out)


def first_row_sums(s, units, dirs, pieces, first):
    return chunked(
        first_row_kernel,
        WIDTH // CHUNK,
        [WHOLE, DIRS] + [WHOLE] * 4 + [ANY],
        WHOLE,
        shape((PEERS, RB, LANES)),
        [pltpu.VMEM((GROUP, LANES), F32)],
    )(s, units, dirs, *pieces, first)


def row_kernel(mass, a0, a1, a2, a3, out):
    scale = col_scale((a0, a1, a2, a3))
    for rb in range(RB):
        out[0, rb : rb + 1, :] = row_part(mass, scale, rb)
    copies(out)


def last_row_kernel(mass, a0, a1, a2, a3, exps, out):
    scale = col_scale((a0, a1, a2, a3))
    for rb in range(RB):
        out[0, rb : rb + 1, :] = row_part(mass, scale, rb)
    out[0, RB : 2 * RB, :] = exps[...]
    copies(out)


def student_kernel(s, r0, r1, r2, r3, protos, exps, hat, sums, dirs):
    j = pl.program_id(0)
    put_dirs(protos, dirs)

    @pl.when(j == 0)
    def _():
        sums[...] = jnp.zeros_like(sums)
        for b, rows in enumerate((r0, r1, r2, r3)):
            hat[own_rows(s, b), :] = unit(rows[...], 1)[0].astype(BF16)

    for q in range(CHUNK // TILE):
        for rb in range(RB):
            part = jnp.exp(dot(hat[block(rb), :], dirs[:, tile(q)]) * (1.0 / STUDENT_TEMP))
            sums[block(rb), :] = sums[block(rb), :] + fold_lanes(part)

    @pl.when(j == pl.num_programs(0) - 1)
    def _():
        for rb in range(RB):
            exps[rb : rb + 1, :] = rows_to_lanes(sums[block(rb), :])


def student_exps(s, rows, protos):
    return chunked(
        student_kernel,
        WIDTH // CHUNK,
        [STUDENT_BLOCK] * NY + [proto_block(CHUNK)],
        [WHOLE, WHOLE],
        [shape((RB, LANES)), shape((GROUP, DEPTH), BF16)],
        [pltpu.VMEM((GROUP, LANES), F32), pltpu.VMEM((DEPTH, CHUNK), BF16)],
    )(s, *rows, protos)


def pick_kernel(s, source, features, first, out):
    me = (s[0] * NY + s[1]) * NC + s[2]
    marks = lax.shift_right_logical(source[...], 8) == me
    local = jnp.bitwise_and(source[...], ROWS - 1).astype(F32)
    counts = exclusive_counts(jnp.where(marks, 1.0, 0.0))
    counts = jnp.where(marks, counts, -1.0)
    rank = lax.broadcasted_iota(jnp.int32, (PARTS, SLOT, ROWS), 1).astype(F32)
    shown = jnp.where(counts[:, None, :] == rank, local[:, None, :], 0.0)
    asked = jnp.sum(shown, axis=2, keepdims=True)
    lane = lax.broadcasted_iota(jnp.int32, (PARTS, SLOT, ROWS), 2).astype(F32)
    pick = jnp.where(asked == lane, 1.0, 0.0).reshape(ROWS, ROWS).astype(BF16)
    rows = dot(pick, features[...])
    for x in range(NX):
        for c in range(NC):
            parts = []
            for y in range(NY):
                e = ((x * NY + y) * NC + c) * SLOT
                parts.append(rows[e : e + SLOT, :])
            parcel = jnp.concatenate(parts, axis=0).astype(BF16)
            for y in range(NY):
                out[(x * NY + y) * NC + c] = parcel


def pick_rows(s, source, features, first):
    return pl.pallas_call(
        pick_kernel,
        in_specs=[pl.BlockSpec(memory_space=pltpu.SMEM), WHOLE, WHOLE, ANY],
        out_specs=WHOLE,
        out_shape=shape((PARTS, NY * SLOT, DEPTH), BF16),
        cost_estimate=COST,
        compiler_params=PARAMS,
    )(s, source, features, first)


def matched_kernel(s, source, arrived, dirs, mass, units):
    j = pl.program_id(0)

    @pl.when(j == 0)
    def _():
        index = lax.broadcasted_iota(jnp.int32, (PARTS, ROWS), 0)
        part = lax.broadcasted_iota(jnp.int32, (PARTS, ROWS), 0)
        slot = lax.broadcasted_iota(jnp.int32, (ROWS, ROWS), 0).astype(F32)
        rows = arrived[...].astype(F32)
        for y in range(NY):
            e = (s[0] * NY + y) * NC + s[2]
            mine = jnp.sum(jnp.where(index == e, source[...], 0), axis=0, keepdims=True)
            owner = lax.shift_right_logical(mine, 8)
            marks = jnp.where(part == owner, 1.0, 0.0)
            rank = jnp.sum(marks * exclusive_counts(marks), axis=0, keepdims=True)
            place = jnp.where(slot == owner.astype(F32) * SLOT + rank, 1.0, 0.0).astype(BF16)
            came = rows[:, y * SLOT : (y + 1) * SLOT, :].reshape(ROWS, DEPTH).astype(BF16)
            matched = lax.dot_general(place, came, (((0,), (0,)), ((), ())), preferred_element_type=F32)
            units[y * ROWS : (y + 1) * ROWS, :] = unit(matched, 1)[0].astype(BF16)

    for q in range(CHUNK // TILE):
        for rb in range(RB):
            mass[block(rb), tile_at(j, q)] = mass_block(units, dirs[:, tile(q)], rb)


def matched_mass(s, source, arrived, dirs):
    return chunked(
        matched_kernel,
        WIDTH // CHUNK,
        [WHOLE, WHOLE, DIRS],
        [WHOLE, WHOLE],
        [shape((GROUP, WIDTH)), shape((GROUP, DEPTH), BF16)],
    )(s, source, arrived, dirs)


def target_kernel(s, mass, a0, a1, a2, a3, got, hat, protos, targets, exps, out, sums, cross, dirs):
    j = pl.program_id(0)
    n = CHUNK // LANES

    @pl.when(j == 0)
    def _():
        sums[...] = jnp.zeros_like(sums)
        cross[...] = jnp.zeros_like(cross)
        exps[...] = jnp.sum(got[...], axis=0)

    put_dirs(protos, dirs)
    rows = pl.ds(pl.multiple_of(j * n, n), n)
    scale = (CROPS / PROTOS) / (a0[rows, :] + a1[rows, :] + a2[rows, :] + a3[rows, :])
    row_scale = 1.0 / (CROPS * exps[:RB, :])
    for rb in range(RB):
        factor = lanes_to_rows(row_scale[rb : rb + 1, :])
        scores = dot(hat[block(rb), :], dirs[...]) * (1.0 / STUDENT_TEMP)
        total = jnp.zeros((LANES, LANES), F32)
        crossed = jnp.zeros((LANES, LANES), F32)
        for k in range(n):
            cols = pl.ds(pl.multiple_of(j * CHUNK + k * LANES, LANES), LANES)
            value = (mass[block(rb), cols] * factor * scale[k : k + 1, :]).astype(BF16)
            targets[block(rb), cols] = value
            value = value.astype(F32)
            total = total + value
            crossed = crossed + value * scores[:, block(k)]
        sums[block(rb), :] = sums[block(rb), :] + total
        cross[...] = cross[...] + crossed

    @pl.when(j == pl.num_programs(0) - 1)
    def _():
        loss = jnp.zeros((1, LANES), F32)
        for rb in range(RB):
            total = rows_to_lanes(sums[block(rb), :])
            out[0, rb : rb + 1, :] = total
            loss = loss + total * jnp.log(exps[RB + rb : RB + rb + 1, :])
        loss = loss - jnp.sum(cross[...], axis=0, keepdims=True)
        out[0, RB : 2 * RB, :] = jnp.broadcast_to(loss, (RB, LANES))
        copies(out)


def make_targets(s, mass, pieces, got, hat, protos):
    return chunked(
        target_kernel,
        WIDTH // CHUNK,
        [WHOLE] * 7 + [proto_block(CHUNK)],
        [WHOLE, WHOLE, WHOLE],
        [
            shape((GROUP, WIDTH), BF16),
            shape((2 * RB, LANES)),
            shape((PEERS, 2 * RB, LANES)),
        ],
        [
            pltpu.VMEM((GROUP, LANES), F32),
            pltpu.VMEM((LANES, LANES), F32),
            pltpu.VMEM((DEPTH, CHUNK), BF16),
        ],
    )(s, mass, *pieces, got, hat, protos)


def grad_kernel(
    s, targets, exps, got, hat, protos, r0, r1, r2, r3, f0, f1, f2, f3, keep, give, loss,
    factor, grads, turned, dirs, feature
):
    j = pl.program_id(0)

    @pl.when(j == 0)
    def _():
        totals = jnp.sum(got[...], axis=0)
        loss[...] = totals[RB:, :]
        scale = totals[:RB, :] / exps[RB:, :]
        for rb in range(RB):
            factor[block(rb), :] = lanes_to_rows(scale[rb : rb + 1, :])
        turned[...] = hat[...].astype(F32).T.astype(BF16)
        feature[...] = jnp.zeros_like(feature)

    put_dirs(protos, dirs)
    for rb in range(RB):
        probs = jnp.exp(dot(hat[block(rb), :], dirs[...]) * (1.0 / STUDENT_TEMP))
        for k in range(GRAD_CHUNK // LANES):
            cols = pl.ds(pl.multiple_of(j * GRAD_CHUNK + k * LANES, LANES), LANES)
            came = targets[block(rb), cols].astype(F32)
            value = probs[:, block(k)] * factor[block(rb), :] - came
            grads[block(rb), block(k)] = (value * (1.0 / STUDENT_TEMP)).astype(BF16)
    feature[...] = feature[...] + lax.dot_general(
        grads[...], dirs[...], (((1,), (1,)), ((), ())), preferred_element_type=F32
    )
    weights = dot(turned[...], grads[...])
    for k in range(GRAD_CHUNK // LANES):
        weight = weights[:, block(k)]
        floats, inverse = unit(protos[:, block(k)], 0)
        stat = jnp.sum(weight * dirs[:, block(k)].astype(F32), axis=0, keepdims=True)
        weight = ((weight - floats * stat) * inverse).reshape(NX * NY, NC, DEPTH // PARTS, LANES)
        own = s[2] == 0
        keep[:, :, block(k)] = jnp.where(own, weight[:, 0], weight[:, 1])
        give[:, :, block(k)] = jnp.where(own, weight[:, 1], weight[:, 0])

    @pl.when(j == pl.num_programs(0) - 1)
    def _():
        for b, (rows, out) in enumerate(((r0, f0), (r1, f1), (r2, f2), (r3, f3))):
            units, inverse = unit(rows[...], 1)
            value = feature[own_rows(s, b), :]
            along = jnp.sum(units * value, axis=1, keepdims=True)
            out[...] = (value - units * along) * inverse


def gradients(s, targets, exps, got, hat, protos, rows):
    share = (NX * NY, DEPTH // PARTS, WIDTH)
    part = pl.BlockSpec((NX * NY, DEPTH // PARTS, GRAD_CHUNK), lambda j, s: (0, 0, j))
    return chunked(
        grad_kernel,
        WIDTH // GRAD_CHUNK,
        [WHOLE, WHOLE, WHOLE, WHOLE, proto_block(GRAD_CHUNK)] + [STUDENT_BLOCK] * NY,
        [WHOLE] * NY + [part, part, WHOLE],
        [shape((ROWS, DEPTH))] * NY + [shape(share), shape(share), shape((RB, LANES))],
        [
            pltpu.VMEM((GROUP, LANES), F32),
            pltpu.VMEM((GROUP, GRAD_CHUNK), BF16),
            pltpu.VMEM((DEPTH, GROUP), BF16),
            pltpu.VMEM((DEPTH, GRAD_CHUNK), BF16),
            pltpu.VMEM((GROUP, DEPTH), F32),
        ],
    )(s, targets, exps, got, hat, protos, *rows)


def add_kernel(s, a, b, first, out):
    out[...] = a[...] + b[...]


def add_shares(s, a, b, first):
    part = pl.BlockSpec((NY, DEPTH // PARTS, WIDTH), lambda j, s: (j, 0, 0))
    return chunked(add_kernel, NX, [part, part, ANY], part, shape(a.shape))(s, a, b, first)


def join_kernel(z, *args):
    out = args[-1]
    rows = args[0].shape[0]
    for b, piece in enumerate(args[:-1]):
        k = lax.rem(z[0] // 2 - b + NZ // 2, NZ // 2) * rows
        out[pl.ds(pl.multiple_of(k, rows), rows), :] = piece[...]


def join_z(z, pieces):
    return pl.pallas_call(
        join_kernel,
        in_specs=[pl.BlockSpec(memory_space=pltpu.SMEM)] + [WHOLE] * len(pieces),
        out_specs=WHOLE,
        out_shape=shape((ROWS, DEPTH)),
        cost_estimate=COST,
        compiler_params=PARAMS,
    )(z, *pieces)


def shift(v, axis, size, step):
    return lax.ppermute(v, axis, [(i, (i + step) % size) for i in range(size)])


def gather_y(v):
    return [v] + [shift(v, "y", NY, b) for b in range(1, NY)]


def swap_rows(v):
    return lax.all_to_all(v, ("y", "z"), 0, 0, tiled=True)


def column_pieces(v):
    v = v + shift(v, "c", NC, 1)
    return [v] + [shift(v, "x", NX, b) for b in range(1, NX)]


def body(teacher_features, teacher_protos, student_features, student_protos, student_source):
    s = jnp.stack([lax.axis_index(a) for a in DP]).astype(jnp.int32)
    teacher_protos = pltpu.with_memory_space_constraint(teacher_protos, pltpu.HBM)
    student_protos = pltpu.with_memory_space_constraint(student_protos, pltpu.HBM)
    source = lax.all_to_all(
        jnp.broadcast_to(student_source[None], (PARTS, ROWS)), DP, 0, 0, tiled=True
    )
    rows = gather_y(jnp.concatenate([teacher_features, student_features], axis=1))
    column, dirs, units = teacher_units(s, rows, teacher_protos)
    got = swap_rows(first_row_sums(s, units, dirs, column_pieces(column), source))

    exps, hat = student_exps(s, rows, student_protos)
    mass, column = columns_again(s, units, dirs, got, [source], 1)
    parts = call(row_kernel, shape((PEERS, RB, LANES)), mass, *column_pieces(column))
    got = swap_rows(parts)

    parcel = pick_rows(s, source, teacher_features, exps)
    arrived = lax.all_to_all(parcel, DP, 0, 0, tiled=True)
    (column,) = columns_again(s, units, dirs, got, [exps], 0)
    mass, _ = matched_mass(s, source, arrived, dirs)
    pieces = column_pieces(column)
    got = swap_rows(call(last_row_kernel, shape((PEERS, 2 * RB, LANES)), mass, *pieces, exps))

    targets, exps, parts = make_targets(s, mass, pieces, got, hat, student_protos)
    got = swap_rows(parts)
    *features, keep, give, loss = gradients(
        s, targets, exps, got, hat, student_protos, rows
    )
    feature = features[0]
    for b in range(1, NY):
        feature = feature + shift(features[b], "y", NY, NY - b)
    feature = lax.all_to_all(feature.reshape(NZ, ROWS // NZ, DEPTH), "z", 0, 0, tiled=True)
    feature = jnp.sum(feature, axis=0)
    loss = functools.reduce(jnp.add, column_pieces(loss))
    weight = add_shares(s, keep, shift(give, "c", NC, 1), loss)
    weight = lax.all_to_all(weight, ("x", "y"), 0, 0, tiled=True)

    z = lax.axis_index("z").astype(jnp.int32).reshape(1)
    other = lax.ppermute(feature, "z", [(i, i ^ 1) for i in range(NZ)])
    even = z[0] % 2 == 0
    pair = jnp.concatenate([jnp.where(even, feature, other), jnp.where(even, other, feature)])
    pieces = [pair] + [shift(pair, "z", NZ, 2 * b) for b in range(1, NZ // 2)]
    grad_features = join_z(z, pieces)

    weight = jnp.sum(weight.reshape(NX, NY, DEPTH // PARTS, WIDTH), axis=0)
    grad_protos = weight.transpose(1, 0, 2).reshape(DEPTH // PARTS, NY * WIDTH)

    loss = jnp.sum(loss[0]) / CROPS
    return (loss, grad_features, grad_protos)


def solution(mesh):
    return jax.shard_map(
        body,
        mesh=Mesh(mesh.devices.reshape(NX, NY, NC, NZ), ("x", "y", "c", "z")),
        in_specs=(P(DP, None), P(None, "z"), P(DP, None), P(None, "z"), P(DP)),
        out_specs=(P(), P(DP, None), P(DP, "z")),
        check_vma=False,
    )
```
